512 devices in a mesh: shot: 32 (over y, x_lo, core), slab: 16 (over z, x_hi).
Axes of the slice: x: 4 (x_hi: 2, x_lo: 2; x = x_hi * 2 + x_lo), y: 8, z: 8, core: 2. Of those that a mesh axis runs over, the one named last changes fastest.
Arguments:
- velocity: float32 [256, 256, 128], P('slab', 'shot'), may hold values from 1.5 to 4.5
- aperture_start: int32 [32], P('shot'), may hold values from 0 to 28, as said below
- aperture_count: int32 [32], P('shot'), may hold values from 1 to 4
- wave_prev: float32 [32, 256, 32, 128], P('shot', 'slab'), may hold values from -6 to 6
- wave_now: float32 [32, 256, 32, 128], P('shot', 'slab'), may hold values from -6 to 6
- adjoint_prev: float32 [32, 256, 32, 128], P('shot', 'slab'), may hold values from -6 to 6
- adjoint_now: float32 [32, 256, 32, 128], P('shot', 'slab'), may hold values from -6 to 6
- source_cells: int32 [32, 4, 3], P('shot'), may hold values from 0 to 255, as said below
- wavelet: float32 [32, 4, 4], P('shot'), may hold values from -6 to 6
- receiver_cells: int32 [32, 16, 3], P('shot'), may hold values from 0 to 255, as said below
- trace: float32 [32, 4, 16], P('shot'), may hold values from -6 to 6
Outputs:
- wave_final: float32 [32, 256, 32, 128], P('shot', 'slab')
- adjoint_final: float32 [32, 256, 32, 128], P('shot', 'slab')
- gradient: float32 [256, 256, 128], P('slab', 'shot')
The draws below stay inside these ranges and needn't reach their ends.
Inputs may be any that keep to these rules, and one draw needn't show every extreme that they name: aperture_start[g] lies between g - 3 and g, and at most 28. `source_cells`: x below 256, window y below 8, z below 128. `receiver_cells`: x below 256, window y below 8, z below 128.
All inputs are finite; a program needn't handle non-finite values.
Results may differ from the reference program's by a relative error of at most 0.0003.
Values sent between devices are 32-bit elements; how exact they have to be, the bound alone decides.
A program may use at most 64 MiB of HBM per device.

```python
import jax
import jax.numpy as jnp
from jax import lax

BY = 8
NZ = 128
APER = 4
STEPS = 4
SRC = 4
REC = 16
GROUPS = 32
NX = 256
NY = 256
WY = 32


def cell_list(key, count):
    key_x, key_y, key_z = jax.random.split(key, 3)
    across = jax.random.randint(key_x, (GROUPS, count), 0, NX)
    inward = jax.random.randint(key_y, (GROUPS, count), 0, BY)
    downward = jax.random.randint(key_z, (GROUPS, count), 0, NZ)
    across = across.at[0, 0].set(NX - 1)
    across = across.at[0, count - 1].set(0)
    downward = downward.at[0, 0].set(NZ - 1)
    return jnp.stack([across, inward, downward], -1).astype(jnp.int32)


def draw_aperture_start(key, part):
    key = jax.random.fold_in(key, 11)
    jitter = jax.random.randint(key, (GROUPS,), 0, APER)
    centre = jnp.arange(GROUPS, dtype=jnp.int32) - (APER - 1) + jitter
    return jnp.clip(centre, 0, GROUPS - APER).astype(jnp.int32)


def draw_aperture_count(key, part):
    key = jax.random.fold_in(key, 12)
    counts = jax.random.randint(key, (GROUPS,), 1, APER + 1)
    return counts.at[0].set(APER).astype(jnp.int32)


def draw_source_cells(key, part):
    key = jax.random.fold_in(key, 13)
    return cell_list(key, SRC)


def draw_receiver_cells(key, part):
    key = jax.random.fold_in(key, 14)
    return cell_list(key, REC)


def level_of(rng, shape, shards, low, largest):
    gain = 1.0
    for axis_at, blocks in shards:
        heights = jax.random.uniform(jax.random.fold_in(jax.random.fold_in(rng, 6), axis_at), (blocks,), jnp.float32, low / len(shards), largest / len(shards))
        gain = gain * jnp.repeat(jnp.exp(heights), shape[axis_at] // blocks).reshape((-1,) + (1,) * (len(shape) - 1 - axis_at))
    return gain


def scatter_about(own_key, dims, width, bound, shards=(), kind=jnp.bfloat16):
    values = width * jax.random.normal(own_key, dims, jnp.float32)
    if shards:
        values = values * level_of(own_key, dims, shards, -0.22, 0.18)
    return jnp.clip(values, -bound, bound).astype(kind)


def setup_inputs(seed: int = 0) -> dict:
    splits = jax.random.split(jax.random.key(seed), 12)
    return {
        "velocity": jnp.clip(1.5 + 3.0 * jax.random.uniform(splits[0], (NX, NY, NZ), jnp.float32) ** level_of(splits[0], (NX, NY, NZ), ((0, 16), (1, 32)), -0.2, 0.2), 1.5, 4.5),
        "aperture_start": draw_aperture_start(jax.random.fold_in(splits[11], 71), 0),
        "aperture_count": draw_aperture_count(jax.random.fold_in(splits[11], 71), 0),
        "wave_prev": scatter_about(splits[3], (GROUPS, NX, WY, NZ), 1.0, 6.0, ((0, 32), (1, 16)), jnp.float32),
        "wave_now": scatter_about(splits[4], (GROUPS, NX, WY, NZ), 1.0, 6.0, ((0, 32), (1, 16)), jnp.float32),
        "adjoint_prev": scatter_about(splits[5], (GROUPS, NX, WY, NZ), 1.0, 6.0, ((0, 32), (1, 16)), jnp.float32),
        "adjoint_now": scatter_about(splits[6], (GROUPS, NX, WY, NZ), 1.0, 6.0, ((0, 32), (1, 16)), jnp.float32),
        "source_cells": draw_source_cells(jax.random.fold_in(splits[11], 71), 0),
        "wavelet": scatter_about(splits[8], (GROUPS, STEPS, SRC), 1.0, 6.0, ((0, 32),), jnp.float32),
        "receiver_cells": draw_receiver_cells(jax.random.fold_in(splits[11], 71), 0),
        "trace": scatter_about(splits[10], (GROUPS, STEPS, REC), 1.0, 6.0, ((0, 32),), jnp.float32),
    }


stencil_weights = (-205.0 / 72.0, 8.0 / 5.0, -1.0 / 5.0, 8.0 / 315.0, -1.0 / 560.0)
time_step = 0.09


def stencil(padded):
    size_x = padded.shape[-3] - 8
    size_y = padded.shape[-2] - 8
    size_z = padded.shape[-1] - 8
    center = padded[..., 4:4 + size_x, 4:4 + size_y, 4:4 + size_z]
    total = (3.0 * stencil_weights[0]) * center
    for k in range(1, 5):
        near = padded[..., 4 + k:4 + k + size_x, 4:4 + size_y, 4:4 + size_z]
        near = near + padded[..., 4 - k:4 - k + size_x, 4:4 + size_y, 4:4 + size_z]
        near = near + padded[..., 4:4 + size_x, 4 + k:4 + k + size_y, 4:4 + size_z]
        near = near + padded[..., 4:4 + size_x, 4 - k:4 - k + size_y, 4:4 + size_z]
        near = near + padded[..., 4:4 + size_x, 4:4 + size_y, 4 + k:4 + k + size_z]
        near = near + padded[..., 4:4 + size_x, 4:4 + size_y, 4 - k:4 - k + size_z]
        total = total + stencil_weights[k] * near
    return total


def inject(cells, amps, x_cells, rows, depth):
    along_x = (x_cells[:, None] == cells[None, :, 0]).astype(jnp.float32) * amps[None, :]
    along_y = (jnp.arange(rows)[:, None] == cells[None, :, 1]).astype(jnp.float32)
    along_z = (jnp.arange(depth)[:, None] == cells[None, :, 2]).astype(jnp.float32)
    return jnp.einsum("xs,ys,zs->xyz", along_x, along_y, along_z, precision=lax.Precision.HIGHEST)


def reference(velocity, aperture_start, aperture_count, wave_prev, wave_now, adjoint_prev, adjoint_now, source_cells, wavelet, receiver_cells, trace):
    rows = APER * BY
    x_cells = jnp.arange(NX)
    zero = jnp.zeros((), jnp.int32)

    def one_group(total, items):
        start_block, live_count, w_prev, w_now, j_prev, j_now, sources, amps, receivers, recorded = items
        anchor = (start_block * BY).astype(jnp.int32)
        window = lax.dynamic_slice(velocity, (zero, anchor, zero), (NX, rows, NZ))
        live = (jnp.arange(rows) < live_count * BY).astype(jnp.float32)[None, :, None]
        courant = window * window * (time_step * time_step)
        imaging = (2.0 * time_step * time_step) * window
        w_prev = w_prev * live
        w_now = w_now * live
        j_prev = j_prev * live
        j_now = j_now * live
        grad = jnp.zeros((NX, rows, NZ), jnp.float32)
        for step in range(STEPS):
            stacked = jnp.stack([w_now, j_now])
            padded = jnp.pad(stacked, ((0, 0), (4, 4), (4, 4), (4, 4)))
            lapl = stencil(padded)
            grad = grad + imaging * j_now * lapl[0]
            w_next = (2.0 * w_now - w_prev + courant * lapl[0] + inject(sources, amps[step], x_cells, rows, NZ)) * live
            j_next = (2.0 * j_now - j_prev + courant * lapl[1] + inject(receivers, recorded[step], x_cells, rows, NZ)) * live
            w_prev, w_now = w_now, w_next
            j_prev, j_now = j_now, j_next
        current = lax.dynamic_slice(total, (zero, anchor, zero), (NX, rows, NZ))
        total = lax.dynamic_update_slice(total, current + grad, (zero, anchor, zero))
        return total, (w_now, j_now)

    begin = jnp.zeros((NX, NY, NZ), jnp.float32)
    gradient, finals = lax.scan(one_group, begin, (aperture_start, aperture_count, wave_prev, wave_now, adjoint_prev, adjoint_now, source_cells, wavelet, receiver_cells, trace))
    return finals[0], finals[1], gradient
```

```python
import functools

import jax
import jax.numpy as jnp
from jax import lax
from jax.experimental import pallas as pl
from jax.experimental.pallas import tpu as pltpu
from jax.sharding import PartitionSpec as P

MESH = pl.DeviceIdType.MESH
STEPS = 4
HALO = 4
PAD = 8
BLOCK = 4
REACH = 3

stencil_weights = (-205.0 / 72.0, 8.0 / 5.0, -1.0 / 5.0, 8.0 / 315.0, -1.0 / 560.0)
time_step = 0.09


def kernel(
    velocity,
    aperture_start,
    aperture_count,
    wave_prev,
    wave_now,
    adjoint_prev,
    adjoint_now,
    source_cells,
    wavelet,
    receiver_cells,
    trace,
    wave_out,
    adjoint_out,
    gradient_out,
    field,
    nearby,
    courant,
    imaging,
    grad,
    spread,
    injected,
    depth_op,
    to_sibling,
    from_sibling,
    to_far,
    from_far,
    to_pair,
    from_pair,
    own_grad,
    load_sem,
    store_sem,
    halo_send,
    halo_recv,
    block_send,
    block_recv,
    grad_send,
    grad_recv,
):
    layers, rows, depth = grad.shape
    brows = velocity.shape[1]
    blocks = rows // brows
    shots, slabs = lax.axis_size("shot"), lax.axis_size("slab")
    shot, slab = lax.axis_index("shot"), lax.axis_index("slab")
    core = lax.rem(shot, 2)
    sibling = shot + 1 - 2 * core
    far = shot - 3 + 6 * core
    has_left, has_right = slab > 0, slab < slabs - 1
    has_far = (far >= 0) & (far < shots)
    has_down, has_up = shot >= 2, shot < shots - 2
    inner = pl.ds(PAD, rows)
    mine = pl.ds(HALO, layers)

    def remote(src, dst, send, recv, where):
        return pltpu.make_async_remote_copy(
            src_ref=src, dst_ref=dst, send_sem=send, recv_sem=recv, device_id=where, device_id_type=MESH
        )

    left, right = {"slab": slab - 1}, {"slab": slab + 1}
    down, up = {"shot": shot - 2}, {"shot": shot + 2}
    partners = (
        (has_left, left),
        (has_right, right),
        (has_down, down),
        (has_up, up),
        (has_far, {"shot": far}),
        (None, {"shot": sibling}),
    )

    def on(condition, action):
        if condition is None:
            action()
        else:
            pl.when(condition)(action)

    loads = [
        pltpu.make_async_copy(wave_now.at[0], field.at[0, 1, mine, inner], load_sem.at[0]),
        pltpu.make_async_copy(adjoint_now.at[0], field.at[1, 1, mine, inner], load_sem.at[1]),
        pltpu.make_async_copy(wave_prev.at[0], field.at[0, 0, mine, inner], load_sem.at[2]),
        pltpu.make_async_copy(adjoint_prev.at[0], field.at[1, 0, mine, inner], load_sem.at[3]),
        pltpu.make_async_copy(velocity, nearby.at[REACH], load_sem.at[4]),
    ]
    for load in loads:
        load.start()

    def clear(edge):
        for f in range(2):
            for t in range(1, STEPS + 1):
                field[f, t, pl.ds(edge, HALO), inner, :] = jnp.zeros((HALO, rows, depth), jnp.float32)

    pl.when(jnp.logical_not(has_left))(lambda: clear(0))
    pl.when(jnp.logical_not(has_right))(lambda: clear(HALO + layers))

    barrier = pltpu.get_barrier_semaphore()
    for condition, where in partners:
        on(condition, lambda where=where: pl.semaphore_signal(barrier, inc=1, device_id=where, device_id_type=MESH))
    peers = 1
    for condition, _ in partners[:-1]:
        peers = peers + condition.astype(jnp.int32)
    pl.semaphore_wait(barrier, peers)

    def halo_copies(f, t, source):
        lo = source.at[pl.ds(0, HALO)] if t == 0 else field.at[f, t + 1, pl.ds(HALO, HALO), inner]
        hi = source.at[pl.ds(layers - HALO, HALO)] if t == 0 else field.at[f, t + 1, pl.ds(layers, HALO), inner]
        return (
            (has_left, has_right, remote(
                lo, field.at[f, t + 1, pl.ds(HALO + layers, HALO), inner],
                halo_send.at[f, t, 0], halo_recv.at[f, t, 0], left)),
            (has_right, has_left, remote(
                hi, field.at[f, t + 1, pl.ds(0, HALO), inner],
                halo_send.at[f, t, 1], halo_recv.at[f, t, 1], right)),
        )

    sources = (wave_now.at[0], adjoint_now.at[0])
    halos = [[halo_copies(f, t, sources[f]) for t in range(STEPS)] for f in range(2)]

    def start_halos(f, t):
        for to, _, copy in halos[f][t]:
            on(to, copy.start)

    def wait_halos(f, t):
        for _, given, copy in halos[f][t]:
            on(given, copy.wait_recv)

    shift = 2 * core - 1 + REACH
    velocity_far = (has_far, remote(
        velocity, nearby.at[6 * (1 - core)], block_send.at[0], block_recv.at[0], {"shot": far}))
    velocity_down = (has_down, has_up, remote(
        velocity, nearby.at[REACH + 2], block_send.at[1], block_recv.at[1], down))
    velocity_up = (has_up, has_down, remote(
        velocity, nearby.at[REACH - 2], block_send.at[2], block_recv.at[2], up))
    sibling_own = remote(velocity, nearby.at[shift], block_send.at[3], block_recv.at[3], {"shot": sibling})
    sibling_low = remote(
        nearby.at[REACH - 2], nearby.at[shift - 2], block_send.at[4], block_recv.at[4], {"shot": sibling})
    sibling_high = remote(
        nearby.at[REACH + 2], nearby.at[shift + 2], block_send.at[5], block_recv.at[5], {"shot": sibling})

    start_halos(0, 0)
    for send in (velocity_down, velocity_up, velocity_far):
        on(send[0], send[-1].start)
    sibling_own.start()
    start_halos(1, 0)

    def clear_rows(i, carry):
        for f in range(2):
            for t in range(1, STEPS + 1):
                field[f, t, HALO + i, pl.ds(0, PAD), :] = jnp.zeros((PAD, depth), jnp.float32)
                field[f, t, HALO + i, pl.ds(PAD + rows, PAD), :] = jnp.zeros((PAD, depth), jnp.float32)
        return carry

    lax.fori_loop(0, layers, clear_rows, 0)

    apart = jnp.abs(
        lax.broadcasted_iota(jnp.int32, (depth, depth), 0) - lax.broadcasted_iota(jnp.int32, (depth, depth), 1)
    )
    operator = jnp.zeros((depth, depth), jnp.float32)
    for k in range(1, HALO + 1):
        operator = jnp.where(apart == k, jnp.float32(stencil_weights[k]), operator)
    op_high = operator.astype(jnp.bfloat16)
    op_low = (operator - op_high.astype(jnp.float32)).astype(jnp.bfloat16)
    for half in range(2):
        depth_op[pl.ds(half * depth, depth), pl.ds(0, depth)] = op_high
        depth_op[pl.ds(half * depth, depth), pl.ds(depth, depth)] = op_low

    at_y = lax.broadcasted_iota(jnp.int32, (PAD, depth), 0)
    at_z = lax.broadcasted_iota(jnp.int32, (PAD, depth), 1)
    first = slab * layers
    for f, (cells, amps) in enumerate(((source_cells, wavelet), (receiver_cells, trace))):
        count = cells.shape[1]

        def inject(x, carry, f=f, cells=cells, amps=amps, count=count):
            sums = [jnp.zeros((PAD, depth), jnp.float32)] * STEPS
            for s in range(count):
                hit = (at_y == cells[0, s, 1]) & (at_z == cells[0, s, 2])
                here = cells[0, s, 0] == first + x
                for t in range(STEPS):
                    amp = jnp.where(here, amps[0, t, s], 0.0)
                    sums[t] = sums[t] + jnp.where(hit, amp, 0.0)
            for t in range(STEPS):
                injected[f, t, x] = sums[t]
            return carry

        lax.fori_loop(0, layers, inject, 0)

    live_rows = aperture_count[0] * brows
    at_row = lax.broadcasted_iota(jnp.int32, (1, rows, depth), 1)
    live = at_row < live_rows

    def keep(f, t, start, size):
        part = field[f, t, pl.ds(start, size), inner, :]
        field[f, t, pl.ds(start, size), inner, :] = jnp.where(live, part, 0.0)

    for i, (f, t) in enumerate(((0, 1), (1, 1), (0, 0), (1, 0))):
        loads[i].wait()
        lax.fori_loop(0, layers // BLOCK, lambda b, c, f=f, t=t: (keep(f, t, HALO + b * BLOCK, BLOCK), c)[1], 0)

    on(velocity_down[1], velocity_down[2].wait_recv)
    on(velocity_up[1], velocity_up[2].wait_recv)
    on(has_down, sibling_low.start)
    on(has_up, sibling_high.start)
    loads[4].wait()
    on(has_far, velocity_far[1].wait_recv)
    sibling_own.wait_recv()
    sib_down, sib_up = sibling >= 2, sibling < shots - 2
    on(sib_down, sibling_low.wait_recv)
    on(sib_up, sibling_high.wait_recv)

    offset = jnp.clip(aperture_start[0] - shot + REACH, 0, REACH)
    for j in range(blocks):
        part = nearby[offset + j]
        here = pl.ds(j * brows, brows)
        alive = j * brows < live_rows
        imaging[:, here, :] = part * jnp.float32(2.0 * time_step * time_step)
        courant[:, here, :] = jnp.where(alive, part * part * jnp.float32(time_step * time_step), 0.0)

    def advance(f, t, x):
        here = pl.ds(HALO + x, BLOCK)
        now = field[f, t + 1, here, inner, :]
        high = now.astype(jnp.bfloat16)
        low = (now - high.astype(jnp.float32)).astype(jnp.bfloat16)
        both = jnp.concatenate([high, low], axis=-1).reshape(BLOCK * rows, 2 * depth)
        along_z = jnp.dot(both, depth_op[...], preferred_element_type=jnp.float32)
        total = (along_z[:, :depth] + along_z[:, depth:]).reshape(BLOCK, rows, depth)
        total = total + jnp.float32(3.0 * stencil_weights[0]) * now
        for k in range(1, HALO + 1):
            near = field[f, t + 1, pl.ds(HALO + x + k, BLOCK), inner, :]
            near = near + field[f, t + 1, pl.ds(HALO + x - k, BLOCK), inner, :]
            near = near + field[f, t + 1, here, pl.ds(PAD + k, rows), :]
            near = near + field[f, t + 1, here, pl.ds(PAD - k, rows), :]
            total = total + jnp.float32(stencil_weights[k]) * near
        own = pl.ds(x, BLOCK)
        if f == 0:
            image = field[1, t + 1, here, inner, :] * total
            grad[own] = image if t == 0 else grad[own] + image
        later = 2.0 * now - field[f, t, here, inner, :] + courant[own] * total
        field[f, t + 2, here, pl.ds(PAD, PAD), :] = later[:, :PAD] + injected[f, t, own]
        field[f, t + 2, here, pl.ds(2 * PAD, rows - PAD), :] = later[:, PAD:]

    def inside(f, t):
        lax.fori_loop(1, layers // BLOCK - 1, lambda b, c: (advance(f, t, b * BLOCK), c)[1], 0)

    def edges(f, t):
        lax.fori_loop(0, 2, lambda b, c: (advance(f, t, b * (layers - BLOCK)), c)[1], 0)

    outs = [
        pltpu.make_async_copy(field.at[0, STEPS + 1, mine, inner], wave_out.at[0], store_sem.at[0]),
        pltpu.make_async_copy(field.at[1, STEPS + 1, mine, inner], adjoint_out.at[0], store_sem.at[1]),
        pltpu.make_async_copy(own_grad, gradient_out, store_sem.at[2]),
    ]

    grad_sibling = remote(to_sibling, from_sibling, grad_send.at[0], grad_recv.at[0], {"shot": sibling})
    grad_far = (has_far, remote(to_far, from_far, grad_send.at[1], grad_recv.at[1], {"shot": far}))
    grad_down = (has_down, has_up, remote(
        to_pair.at[0], from_pair.at[1], grad_send.at[2], grad_recv.at[2], down))
    grad_up = (has_up, has_down, remote(
        to_pair.at[1], from_pair.at[0], grad_send.at[3], grad_recv.at[3], up))
    back = 2 * REACH - offset

    def piece(o):
        return spread[back + o]

    def send_gradient():
        for j in range(REACH):
            spread[j] = jnp.zeros(spread.shape[1:], jnp.float32)
            spread[REACH + blocks + j] = jnp.zeros(spread.shape[1:], jnp.float32)
        for j in range(blocks):
            here = pl.ds(j * brows, brows)
            spread[REACH + j] = grad[:, here, :] * imaging[:, here, :]
        toward = 1 - 2 * core
        for i, o in enumerate((0, -2, 2)):
            to_sibling[i] = piece(toward + o)
        grad_sibling.start()
        to_far[...] = piece(6 * core - 3)
        on(has_far, grad_far[1].start)

    def pass_gradient():
        grad_sibling.wait_recv()
        to_pair[0] = piece(-2) + from_sibling[1]
        to_pair[1] = piece(2) + from_sibling[2]
        on(has_down, grad_down[2].start)
        on(has_up, grad_up[2].start)

    def take_gradient():
        total = piece(0) + from_sibling[0]
        on(has_far, grad_far[1].wait_recv)
        on(has_up, grad_down[2].wait_recv)
        on(has_down, grad_up[2].wait_recv)
        total = total + jnp.where(has_far, from_far[...], 0.0)
        total = total + jnp.where(has_down, from_pair[0], 0.0)
        total = total + jnp.where(has_up, from_pair[1], 0.0)
        own_grad[...] = total

    def mask_halos(f):
        keep(f, 1, 0, HALO)
        keep(f, 1, HALO + layers, HALO)

    for t in range(STEPS):
        last = t == STEPS - 1
        inside(0, t)
        wait_halos(0, t)
        if t == 0:
            mask_halos(0)
        edges(0, t)
        if last:
            outs[0].start()
            send_gradient()
        else:
            start_halos(0, t + 1)
        inside(1, t)
        if last:
            pass_gradient()
        wait_halos(1, t)
        if t == 0:
            mask_halos(1)
        edges(1, t)
        if last:
            outs[1].start()
        else:
            start_halos(1, t + 1)
    take_gradient()
    outs[2].start()

    for f in range(2):
        for t in range(STEPS):
            for to, _, copy in halos[f][t]:
                on(to, copy.wait_send)
    for send in (velocity_far, velocity_down, velocity_up, grad_far, grad_down, grad_up):
        on(send[0], send[-1].wait_send)
    sibling_own.wait_send()
    on(has_down, sibling_low.wait_send)
    on(has_up, sibling_high.wait_send)
    grad_sibling.wait_send()
    for out in outs:
        out.wait()


def per_device(*args):
    velocity, wave_now = args[0], args[4]
    layers, brows, depth = velocity.shape
    rows = wave_now.shape[2]
    blocks = rows // brows
    block = (layers, brows, depth)
    anywhere = pl.BlockSpec(memory_space=pl.ANY)
    scalars = pl.BlockSpec(memory_space=pltpu.SMEM)
    f32 = jnp.float32
    return pl.pallas_call(
        kernel,
        out_shape=(
            jax.ShapeDtypeStruct(wave_now.shape, f32),
            jax.ShapeDtypeStruct(wave_now.shape, f32),
            jax.ShapeDtypeStruct(velocity.shape, f32),
        ),
        in_specs=[anywhere, scalars, scalars] + [anywhere] * 4 + [scalars] * 4,
        out_specs=(anywhere,) * 3,
        scratch_shapes=[
            pltpu.VMEM((2, STEPS + 2, layers + 2 * HALO, rows + 2 * PAD, depth), f32),
            pltpu.VMEM((2 * REACH + 1, *block), f32),
            pltpu.VMEM((layers, rows, depth), f32),
            pltpu.VMEM((layers, rows, depth), f32),
            pltpu.VMEM((layers, rows, depth), f32),
            pltpu.VMEM((blocks + 2 * REACH, *block), f32),
            pltpu.VMEM((2, STEPS, layers, PAD, depth), f32),
            pltpu.VMEM((2 * depth, 2 * depth), jnp.bfloat16),
            pltpu.VMEM((3, *block), f32),
            pltpu.VMEM((3, *block), f32),
            pltpu.VMEM(block, f32),
            pltpu.VMEM(block, f32),
            pltpu.VMEM((2, *block), f32),
            pltpu.VMEM((2, *block), f32),
            pltpu.VMEM(block, f32),
            pltpu.SemaphoreType.DMA((5,)),
            pltpu.SemaphoreType.DMA((3,)),
            pltpu.SemaphoreType.DMA((2, STEPS, 2)),
            pltpu.SemaphoreType.DMA((2, STEPS, 2)),
            pltpu.SemaphoreType.DMA((6,)),
            pltpu.SemaphoreType.DMA((6,)),
            pltpu.SemaphoreType.DMA((4,)),
            pltpu.SemaphoreType.DMA((4,)),
        ],
        compiler_params=pltpu.CompilerParams(
            collective_id=0, has_side_effects=True, vmem_limit_bytes=60 * 1024 * 1024
        ),
        name="inversion",
    )(*args)


def solution(mesh):
    fields = P("shot", "slab", None, None)
    table = P("shot", None, None)
    return jax.shard_map(
        per_device,
        mesh=mesh,
        in_specs=(P("slab", "shot", None), P("shot"), P("shot"), fields, fields, fields, fields, table, table, table, table),
        out_specs=(fields, fields, P("slab", "shot", None)),
        check_vma=False,
    )
```

```python
import functools

import jax
import jax.numpy as jnp
from jax import lax
from jax.experimental import pallas as pl
from jax.experimental.pallas import tpu as pltpu
from jax.sharding import PartitionSpec as P

MESH = pl.DeviceIdType.MESH
STEPS = 4
HALO = 4
PAD = 8
BLOCK = 4
REACH = 3

stencil_weights = (-205.0 / 72.0, 8.0 / 5.0, -1.0 / 5.0, 8.0 / 315.0, -1.0 / 560.0)
time_step = 0.09


def kernel(
    velocity,
    aperture_start,
    aperture_count,
    wave_prev,
    wave_now,
    adjoint_prev,
    adjoint_now,
    source_cells,
    wavelet,
    receiver_cells,
    trace,
    wave_out,
    adjoint_out,
    gradient_out,
    field,
    nearby,
    courant,
    imaging,
    grad,
    spread,
    injected,
    depth_op,
    to_sibling,
    from_sibling,
    to_far,
    from_far,
    to_pair,
    from_pair,
    load_sem,
    halo_send,
    halo_recv,
    block_send,
    block_recv,
    grad_send,
    grad_recv,
):
    layers, rows, depth = grad.shape
    brows = velocity.shape[1]
    blocks = rows // brows
    shots, slabs = lax.axis_size("shot"), lax.axis_size("slab")
    shot, slab = lax.axis_index("shot"), lax.axis_index("slab")
    core = lax.rem(shot, 2)
    sibling = shot + 1 - 2 * core
    far = shot - 3 + 6 * core
    has_left, has_right = slab > 0, slab < slabs - 1
    has_far = (far >= 0) & (far < shots)
    has_down, has_up = shot >= 2, shot < shots - 2
    inner = pl.ds(PAD, rows)
    mine = pl.ds(HALO, layers)

    def remote(src, dst, send, recv, where):
        return pltpu.make_async_remote_copy(
            src_ref=src, dst_ref=dst, send_sem=send, recv_sem=recv, device_id=where, device_id_type=MESH
        )

    left, right = {"slab": slab - 1}, {"slab": slab + 1}
    down, up = {"shot": shot - 2}, {"shot": shot + 2}
    partners = (
        (has_left, left),
        (has_right, right),
        (has_down, down),
        (has_up, up),
        (has_far, {"shot": far}),
        (None, {"shot": sibling}),
    )

    def on(condition, action):
        if condition is None:
            action()
        else:
            pl.when(condition)(action)

    loads = [
        pltpu.make_async_copy(wave_now.at[0], field.at[0, 1, mine, inner], load_sem.at[0]),
        pltpu.make_async_copy(adjoint_now.at[0], field.at[1, 1, mine, inner], load_sem.at[1]),
        pltpu.make_async_copy(wave_prev.at[0], field.at[0, 0, mine, inner], load_sem.at[2]),
        pltpu.make_async_copy(adjoint_prev.at[0], field.at[1, 0, mine, inner], load_sem.at[3]),
        pltpu.make_async_copy(velocity, nearby.at[REACH], load_sem.at[4]),
    ]
    for load in loads:
        load.start()

    def clear(edge):
        for f in range(2):
            for t in range(1, STEPS + 1):
                field[f, t, pl.ds(edge, HALO), inner, :] = jnp.zeros((HALO, rows, depth), jnp.float32)

    pl.when(jnp.logical_not(has_left))(lambda: clear(0))
    pl.when(jnp.logical_not(has_right))(lambda: clear(HALO + layers))

    barrier = pltpu.get_barrier_semaphore()
    for condition, where in partners:
        on(condition, lambda where=where: pl.semaphore_signal(barrier, inc=1, device_id=where, device_id_type=MESH))
    peers = 1
    for condition, _ in partners[:-1]:
        peers = peers + condition.astype(jnp.int32)
    pl.semaphore_wait(barrier, peers)

    def halo_copies(f, t, source):
        lo = source.at[pl.ds(0, HALO)] if t == 0 else field.at[f, t + 1, pl.ds(HALO, HALO), inner]
        hi = source.at[pl.ds(layers - HALO, HALO)] if t == 0 else field.at[f, t + 1, pl.ds(layers, HALO), inner]
        return (
            (has_left, has_right, remote(
                lo, field.at[f, t + 1, pl.ds(HALO + layers, HALO), inner],
                halo_send.at[f, t, 0], halo_recv.at[f, t, 0], left)),
            (has_right, has_left, remote(
                hi, field.at[f, t + 1, pl.ds(0, HALO), inner],
                halo_send.at[f, t, 1], halo_recv.at[f, t, 1], right)),
        )

    sources = (wave_now.at[0], adjoint_now.at[0])
    halos = [[halo_copies(f, t, sources[f]) for t in range(STEPS)] for f in range(2)]

    def start_halos(f, t):
        for to, _, copy in halos[f][t]:
            on(to, copy.start)

    def wait_halos(f, t):
        for _, given, copy in halos[f][t]:
            on(given, copy.wait_recv)

    shift = 2 * core - 1 + REACH
    velocity_far = (has_far, remote(
        velocity, nearby.at[6 * (1 - core)], block_send.at[0], block_recv.at[0], {"shot": far}))
    velocity_down = (has_down, has_up, remote(
        velocity, nearby.at[REACH + 2], block_send.at[1], block_recv.at[1], down))
    velocity_up = (has_up, has_down, remote(
        velocity, nearby.at[REACH - 2], block_send.at[2], block_recv.at[2], up))
    sibling_own = remote(velocity, nearby.at[shift], block_send.at[3], block_recv.at[3], {"shot": sibling})
    sibling_low = remote(
        nearby.at[REACH - 2], nearby.at[shift - 2], block_send.at[4], block_recv.at[4], {"shot": sibling})
    sibling_high = remote(
        nearby.at[REACH + 2], nearby.at[shift + 2], block_send.at[5], block_recv.at[5], {"shot": sibling})

    start_halos(0, 0)
    for send in (velocity_down, velocity_up, velocity_far):
        on(send[0], send[-1].start)
    sibling_own.start()
    start_halos(1, 0)

    def clear_rows(i, carry):
        for f in range(2):
            for t in range(1, STEPS + 1):
                field[f, t, HALO + i, pl.ds(0, PAD), :] = jnp.zeros((PAD, depth), jnp.float32)
                field[f, t, HALO + i, pl.ds(PAD + rows, PAD), :] = jnp.zeros((PAD, depth), jnp.float32)
        return carry

    lax.fori_loop(0, layers, clear_rows, 0)

    apart = jnp.abs(
        lax.broadcasted_iota(jnp.int32, (depth, depth), 0) - lax.broadcasted_iota(jnp.int32, (depth, depth), 1)
    )
    operator = jnp.zeros((depth, depth), jnp.float32)
    for k in range(1, HALO + 1):
        operator = jnp.where(apart == k, jnp.float32(stencil_weights[k]), operator)
    op_high = operator.astype(jnp.bfloat16)
    op_low = (operator - op_high.astype(jnp.float32)).astype(jnp.bfloat16)
    for half in range(2):
        depth_op[pl.ds(half * depth, depth), pl.ds(0, depth)] = op_high
        depth_op[pl.ds(half * depth, depth), pl.ds(depth, depth)] = op_low

    at_y = lax.broadcasted_iota(jnp.int32, (PAD, depth), 0)
    at_z = lax.broadcasted_iota(jnp.int32, (PAD, depth), 1)
    first = slab * layers
    for f, (cells, amps) in enumerate(((source_cells, wavelet), (receiver_cells, trace))):
        count = cells.shape[-1]

        def inject(x, carry, f=f, cells=cells, amps=amps, count=count):
            sums = [jnp.zeros((PAD, depth), jnp.float32)] * STEPS
            for s in range(count):
                hit = (at_y == cells[1, 0, s]) & (at_z == cells[2, 0, s])
                here = cells[0, 0, s] == first + x
                for t in range(STEPS):
                    amp = jnp.where(here, amps[0, t, s], 0.0)
                    sums[t] = sums[t] + jnp.where(hit, amp, 0.0)
            for t in range(STEPS):
                injected[f, t, x] = sums[t]
            return carry

        lax.fori_loop(0, layers, inject, 0)

    live_rows = aperture_count[0] * brows
    at_row = lax.broadcasted_iota(jnp.int32, (1, rows, depth), 1)
    live = at_row < live_rows

    def keep(f, t, start, size):
        part = field[f, t, pl.ds(start, size), inner, :]
        field[f, t, pl.ds(start, size), inner, :] = jnp.where(live, part, 0.0)

    for i, (f, t) in enumerate(((0, 1), (1, 1), (0, 0), (1, 0))):
        loads[i].wait()
        lax.fori_loop(0, layers // BLOCK, lambda b, c, f=f, t=t: (keep(f, t, HALO + b * BLOCK, BLOCK), c)[1], 0)

    on(velocity_down[1], velocity_down[2].wait_recv)
    on(velocity_up[1], velocity_up[2].wait_recv)
    on(has_down, sibling_low.start)
    on(has_up, sibling_high.start)
    loads[4].wait()
    on(has_far, velocity_far[1].wait_recv)
    sibling_own.wait_recv()
    sib_down, sib_up = sibling >= 2, sibling < shots - 2
    on(sib_down, sibling_low.wait_recv)
    on(sib_up, sibling_high.wait_recv)

    offset = jnp.clip(aperture_start[0] - shot + REACH, 0, REACH)
    for j in range(blocks):
        part = nearby[offset + j]
        here = pl.ds(j * brows, brows)
        alive = j * brows < live_rows
        imaging[:, here, :] = part * jnp.float32(2.0 * time_step * time_step)
        courant[:, here, :] = jnp.where(alive, part * part * jnp.float32(time_step * time_step), 0.0)

    def advance(f, t, x):
        here = pl.ds(HALO + x, BLOCK)
        now = field[f, t + 1, here, inner, :]
        high = now.astype(jnp.bfloat16)
        low = (now - high.astype(jnp.float32)).astype(jnp.bfloat16)
        both = jnp.concatenate([high, low], axis=-1).reshape(BLOCK * rows, 2 * depth)
        along_z = jnp.dot(both, depth_op[...], preferred_element_type=jnp.float32)
        total = (along_z[:, :depth] + along_z[:, depth:]).reshape(BLOCK, rows, depth)
        total = total + jnp.float32(3.0 * stencil_weights[0]) * now
        for k in range(1, HALO + 1):
            near = field[f, t + 1, pl.ds(HALO + x + k, BLOCK), inner, :]
            near = near + field[f, t + 1, pl.ds(HALO + x - k, BLOCK), inner, :]
            near = near + field[f, t + 1, here, pl.ds(PAD + k, rows), :]
            near = near + field[f, t + 1, here, pl.ds(PAD - k, rows), :]
            total = total + jnp.float32(stencil_weights[k]) * near
        own = pl.ds(x, BLOCK)
        if t == STEPS - 1:
            kept, at, row = (wave_out, adjoint_out)[f].at[0], own, 0
        else:
            kept, at, row = field.at[f, t + 2], here, PAD
        if f == 0:
            image = field[1, t + 1, here, inner, :] * total
            grad[own] = image if t == 0 else grad[own] + image
        later = 2.0 * now - field[f, t, here, inner, :] + courant[own] * total
        kept[at, pl.ds(row, PAD), :] = later[:, :PAD] + injected[f, t, own]
        kept[at, pl.ds(row + PAD, rows - PAD), :] = later[:, PAD:]

    def inside(f, t):
        lax.fori_loop(1, layers // BLOCK - 1, lambda b, c: (advance(f, t, b * BLOCK), c)[1], 0)

    def edges(f, t):
        lax.fori_loop(0, 2, lambda b, c: (advance(f, t, b * (layers - BLOCK)), c)[1], 0)

    grad_sibling = remote(to_sibling, from_sibling, grad_send.at[0], grad_recv.at[0], {"shot": sibling})
    grad_far = (has_far, remote(to_far, from_far, grad_send.at[1], grad_recv.at[1], {"shot": far}))
    grad_down = (has_down, has_up, remote(
        to_pair.at[0], from_pair.at[1], grad_send.at[2], grad_recv.at[2], down))
    grad_up = (has_up, has_down, remote(
        to_pair.at[1], from_pair.at[0], grad_send.at[3], grad_recv.at[3], up))
    back = 2 * REACH - offset

    def piece(o):
        return spread[back + o]

    def send_gradient():
        for j in range(REACH):
            spread[j] = jnp.zeros(spread.shape[1:], jnp.float32)
            spread[REACH + blocks + j] = jnp.zeros(spread.shape[1:], jnp.float32)
        for j in range(blocks):
            here = pl.ds(j * brows, brows)
            spread[REACH + j] = grad[:, here, :] * imaging[:, here, :]
        toward = 1 - 2 * core
        for i, o in enumerate((0, -2, 2)):
            to_sibling[i] = piece(toward + o)
        grad_sibling.start()
        to_far[...] = piece(6 * core - 3)
        on(has_far, grad_far[1].start)

    def pass_gradient():
        grad_sibling.wait_recv()
        to_pair[0] = piece(-2) + from_sibling[1]
        to_pair[1] = piece(2) + from_sibling[2]
        on(has_down, grad_down[2].start)
        on(has_up, grad_up[2].start)

    def take_gradient():
        total = piece(0) + from_sibling[0]
        on(has_far, grad_far[1].wait_recv)
        on(has_up, grad_down[2].wait_recv)
        on(has_down, grad_up[2].wait_recv)
        total = total + jnp.where(has_far, from_far[...], 0.0)
        total = total + jnp.where(has_down, from_pair[0], 0.0)
        total = total + jnp.where(has_up, from_pair[1], 0.0)
        gradient_out[...] = total

    def mask_halos(f):
        keep(f, 1, 0, HALO)
        keep(f, 1, HALO + layers, HALO)

    for t in range(STEPS):
        last = t == STEPS - 1
        inside(0, t)
        wait_halos(0, t)
        if t == 0:
            mask_halos(0)
        edges(0, t)
        if last:
            send_gradient()
        else:
            start_halos(0, t + 1)
        inside(1, t)
        if last:
            pass_gradient()
        wait_halos(1, t)
        if t == 0:
            mask_halos(1)
        edges(1, t)
        if not last:
            start_halos(1, t + 1)
    take_gradient()

    for f in range(2):
        for t in range(STEPS):
            for to, _, copy in halos[f][t]:
                on(to, copy.wait_send)
    for send in (velocity_far, velocity_down, velocity_up, grad_far, grad_down, grad_up):
        on(send[0], send[-1].wait_send)
    sibling_own.wait_send()
    on(has_down, sibling_low.wait_send)
    on(has_up, sibling_high.wait_send)
    grad_sibling.wait_send()


def deliver(*refs):
    count = len(refs) // 2
    done = refs[-1]
    copies = [pltpu.make_async_copy(refs[i], refs[count + i], done.at[i]) for i in range(count)]
    for copy in copies:
        copy.start()
    for copy in copies:
        copy.wait()


def per_device(
    velocity,
    aperture_start,
    aperture_count,
    wave_prev,
    wave_now,
    adjoint_prev,
    adjoint_now,
    source_cells,
    wavelet,
    receiver_cells,
    trace,
):
    layers, brows, depth = velocity.shape
    rows = wave_now.shape[2]
    blocks = rows // brows
    block = (layers, brows, depth)
    anywhere = pl.BlockSpec(memory_space=pl.ANY)
    scalars = pl.BlockSpec(memory_space=pltpu.SMEM)
    f32 = jnp.float32
    out_shape = (
        jax.ShapeDtypeStruct(wave_now.shape, f32),
        jax.ShapeDtypeStruct(wave_now.shape, f32),
        jax.ShapeDtypeStruct(velocity.shape, f32),
    )
    results = pl.pallas_call(
        kernel,
        out_shape=tuple(pltpu.VMEM(leaf.shape, leaf.dtype) for leaf in out_shape),
        in_specs=[anywhere, scalars, scalars] + [anywhere] * 4 + [scalars] * 4,
        out_specs=(pl.BlockSpec(memory_space=pltpu.VMEM),) * 3,
        scratch_shapes=[
            pltpu.VMEM((2, STEPS + 1, layers + 2 * HALO, rows + 2 * PAD, depth), f32),
            pltpu.VMEM((2 * REACH + 1, *block), f32),
            pltpu.VMEM((layers, rows, depth), f32),
            pltpu.VMEM((layers, rows, depth), f32),
            pltpu.VMEM((layers, rows, depth), f32),
            pltpu.VMEM((blocks + 2 * REACH, *block), f32),
            pltpu.VMEM((2, STEPS, layers, PAD, depth), f32),
            pltpu.VMEM((2 * depth, 2 * depth), jnp.bfloat16),
            pltpu.VMEM((3, *block), f32),
            pltpu.VMEM((3, *block), f32),
            pltpu.VMEM(block, f32),
            pltpu.VMEM(block, f32),
            pltpu.VMEM((2, *block), f32),
            pltpu.VMEM((2, *block), f32),
            pltpu.SemaphoreType.DMA((5,)),
            pltpu.SemaphoreType.DMA((2, STEPS, 2)),
            pltpu.SemaphoreType.DMA((2, STEPS, 2)),
            pltpu.SemaphoreType.DMA((6,)),
            pltpu.SemaphoreType.DMA((6,)),
            pltpu.SemaphoreType.DMA((4,)),
            pltpu.SemaphoreType.DMA((4,)),
        ],
        compiler_params=pltpu.CompilerParams(
            collective_id=0, has_side_effects=True, vmem_limit_bytes=60 * 1024 * 1024
        ),
        name="inversion",
    )(
        velocity,
        aperture_start,
        aperture_count,
        wave_prev,
        wave_now,
        adjoint_prev,
        adjoint_now,
        jnp.transpose(source_cells, (2, 0, 1)),
        wavelet,
        jnp.transpose(receiver_cells, (2, 0, 1)),
        trace,
    )
    return pl.pallas_call(
        deliver,
        out_shape=out_shape,
        in_specs=[pl.BlockSpec(memory_space=pltpu.VMEM)] * 3,
        out_specs=(anywhere,) * 3,
        scratch_shapes=[pltpu.SemaphoreType.DMA((3,))],
        compiler_params=pltpu.CompilerParams(vmem_limit_bytes=1024 * 1024),
        name="deliver",
    )(*results)


def solution(mesh):
    fields = P("shot", "slab", None, None)
    table = P("shot", None, None)
    return jax.shard_map(
        per_device,
        mesh=mesh,
        in_specs=(P("slab", "shot", None), P("shot"), P("shot"), fields, fields, fields, fields, table, table, table, table),
        out_specs=(fields, fields, P("slab", "shot", None)),
        check_vma=False,
    )
```

```python
import functools

import jax
import jax.numpy as jnp
from jax import lax
from jax.experimental import pallas as pl
from jax.experimental.pallas import tpu as pltpu
from jax.sharding import PartitionSpec as P

MESH = pl.DeviceIdType.MESH
STEPS = 4
HALO = 4
PAD = 8
BLOCK = 4
REACH = 3

stencil_weights = (-205.0 / 72.0, 8.0 / 5.0, -1.0 / 5.0, 8.0 / 315.0, -1.0 / 560.0)
time_step = 0.09


def kernel(
    velocity,
    aperture_start_in,
    aperture_count_in,
    wave_prev,
    wave_now,
    adjoint_prev,
    adjoint_now,
    source_cells_in,
    wavelet_in,
    receiver_cells_in,
    trace_in,
    wave_out,
    adjoint_out,
    gradient_out,
    aperture_start,
    aperture_count,
    source_cells,
    wavelet,
    receiver_cells,
    trace,
    field,
    nearby,
    courant,
    imaging,
    grad,
    spread,
    injected,
    depth_op,
    to_sibling,
    from_sibling,
    to_far,
    from_far,
    to_pair,
    from_pair,
    load_sem,
    table_sem,
    halo_send,
    halo_recv,
    block_send,
    block_recv,
    grad_send,
    grad_recv,
):
    layers, rows, depth = grad.shape
    brows = velocity.shape[1]
    blocks = rows // brows
    shots, slabs = lax.axis_size("shot"), lax.axis_size("slab")
    shot, slab = lax.axis_index("shot"), lax.axis_index("slab")
    core = lax.rem(shot, 2)
    sibling = shot + 1 - 2 * core
    far = shot - 3 + 6 * core
    has_left, has_right = slab > 0, slab < slabs - 1
    has_far = (far >= 0) & (far < shots)
    has_down, has_up = shot >= 2, shot < shots - 2
    inner = pl.ds(PAD, rows)
    mine = pl.ds(HALO, layers)

    def remote(src, dst, send, recv, where):
        return pltpu.make_async_remote_copy(
            src_ref=src, dst_ref=dst, send_sem=send, recv_sem=recv, device_id=where, device_id_type=MESH
        )

    left, right = {"slab": slab - 1}, {"slab": slab + 1}
    down, up = {"shot": shot - 2}, {"shot": shot + 2}
    partners = (
        (has_left, left),
        (has_right, right),
        (has_down, down),
        (has_up, up),
        (has_far, {"shot": far}),
        (None, {"shot": sibling}),
    )

    def on(condition, action):
        if condition is None:
            action()
        else:
            pl.when(condition)(action)

    loads = [
        pltpu.make_async_copy(wave_now.at[0], field.at[0, 1, mine, inner], load_sem.at[0]),
        pltpu.make_async_copy(adjoint_now.at[0], field.at[1, 1, mine, inner], load_sem.at[1]),
        pltpu.make_async_copy(wave_prev.at[0], field.at[0, 0, mine, inner], load_sem.at[2]),
        pltpu.make_async_copy(adjoint_prev.at[0], field.at[1, 0, mine, inner], load_sem.at[3]),
        pltpu.make_async_copy(velocity, nearby.at[REACH], load_sem.at[4]),
    ]
    for load in loads:
        load.start()
    tables = [
        pltpu.make_async_copy(table, held, table_sem.at[i])
        for i, (table, held) in enumerate((
            (aperture_start_in, aperture_start),
            (aperture_count_in, aperture_count),
            (source_cells_in, source_cells),
            (wavelet_in, wavelet),
            (receiver_cells_in, receiver_cells),
            (trace_in, trace),
        ))
    ]
    for table in tables:
        table.start()

    def clear(edge):
        for f in range(2):
            for t in range(1, STEPS + 1):
                field[f, t, pl.ds(edge, HALO), inner, :] = jnp.zeros((HALO, rows, depth), jnp.float32)

    pl.when(jnp.logical_not(has_left))(lambda: clear(0))
    pl.when(jnp.logical_not(has_right))(lambda: clear(HALO + layers))

    barrier = pltpu.get_barrier_semaphore()
    for condition, where in partners:
        on(condition, lambda where=where: pl.semaphore_signal(barrier, inc=1, device_id=where, device_id_type=MESH))
    peers = 1
    for condition, _ in partners[:-1]:
        peers = peers + condition.astype(jnp.int32)
    pl.semaphore_wait(barrier, peers)

    def halo_copies(f, t, source):
        lo = source.at[pl.ds(0, HALO)] if t == 0 else field.at[f, t + 1, pl.ds(HALO, HALO), inner]
        hi = source.at[pl.ds(layers - HALO, HALO)] if t == 0 else field.at[f, t + 1, pl.ds(layers, HALO), inner]
        return (
            (has_left, has_right, remote(
                lo, field.at[f, t + 1, pl.ds(HALO + layers, HALO), inner],
                halo_send.at[f, t, 0], halo_recv.at[f, t, 0], left)),
            (has_right, has_left, remote(
                hi, field.at[f, t + 1, pl.ds(0, HALO), inner],
                halo_send.at[f, t, 1], halo_recv.at[f, t, 1], right)),
        )

    sources = (wave_now.at[0], adjoint_now.at[0])
    halos = [[halo_copies(f, t, sources[f]) for t in range(STEPS)] for f in range(2)]

    def start_halos(f, t):
        for to, _, copy in halos[f][t]:
            on(to, copy.start)

    def wait_halos(f, t):
        for _, given, copy in halos[f][t]:
            on(given, copy.wait_recv)

    shift = 2 * core - 1 + REACH
    velocity_far = (has_far, remote(
        velocity, nearby.at[6 * (1 - core)], block_send.at[0], block_recv.at[0], {"shot": far}))
    velocity_down = (has_down, has_up, remote(
        velocity, nearby.at[REACH + 2], block_send.at[1], block_recv.at[1], down))
    velocity_up = (has_up, has_down, remote(
        velocity, nearby.at[REACH - 2], block_send.at[2], block_recv.at[2], up))
    sibling_own = remote(velocity, nearby.at[shift], block_send.at[3], block_recv.at[3], {"shot": sibling})
    sibling_low = remote(
        nearby.at[REACH - 2], nearby.at[shift - 2], block_send.at[4], block_recv.at[4], {"shot": sibling})
    sibling_high = remote(
        nearby.at[REACH + 2], nearby.at[shift + 2], block_send.at[5], block_recv.at[5], {"shot": sibling})

    for send in (velocity_down, velocity_up, velocity_far):
        on(send[0], send[-1].start)
    sibling_own.start()
    start_halos(0, 0)
    start_halos(1, 0)

    def clear_rows(i, carry):
        for f in range(2):
            for t in range(1, STEPS + 1):
                field[f, t, HALO + i, pl.ds(0, PAD), :] = jnp.zeros((PAD, depth), jnp.float32)
                field[f, t, HALO + i, pl.ds(PAD + rows, PAD), :] = jnp.zeros((PAD, depth), jnp.float32)
        return carry

    lax.fori_loop(0, layers, clear_rows, 0)
    for h in range(2):
        for j in range(REACH):
            spread[h, j] = jnp.zeros(spread.shape[2:], jnp.float32)
            spread[h, REACH + blocks + j] = jnp.zeros(spread.shape[2:], jnp.float32)

    apart = jnp.abs(
        lax.broadcasted_iota(jnp.int32, (depth, depth), 0) - lax.broadcasted_iota(jnp.int32, (depth, depth), 1)
    )
    operator = jnp.zeros((depth, depth), jnp.float32)
    for k in range(1, HALO + 1):
        operator = jnp.where(apart == k, jnp.float32(stencil_weights[k]), operator)
    op_high = operator.astype(jnp.bfloat16)
    op_low = (operator - op_high.astype(jnp.float32)).astype(jnp.bfloat16)
    for half in range(2):
        depth_op[pl.ds(half * depth, depth), pl.ds(0, depth)] = op_high
        depth_op[pl.ds(half * depth, depth), pl.ds(depth, depth)] = op_low

    for table in tables:
        table.wait()
    at_y = lax.broadcasted_iota(jnp.int32, (PAD, depth), 0)
    at_z = lax.broadcasted_iota(jnp.int32, (PAD, depth), 1)
    first = slab * layers
    for f, (cells, amps) in enumerate(((source_cells, wavelet), (receiver_cells, trace))):
        count = cells.shape[-1]

        def inject(x, carry, f=f, cells=cells, amps=amps, count=count):
            sums = [jnp.zeros((PAD, depth), jnp.float32)] * STEPS
            for s in range(count):
                hit = (at_y == cells[1, 0, s]) & (at_z == cells[2, 0, s])
                here = cells[0, 0, s] == first + x
                for t in range(STEPS):
                    amp = jnp.where(here, amps[0, t, s], 0.0)
                    sums[t] = sums[t] + jnp.where(hit, amp, 0.0)
            for t in range(STEPS):
                injected[f, t, x] = sums[t]
            return carry

        lax.fori_loop(0, layers, inject, 0)

    live_rows = aperture_count[0] * brows
    at_row = lax.broadcasted_iota(jnp.int32, (1, rows, depth), 1)
    live = at_row < live_rows

    def keep(f, t, start, size):
        part = field[f, t, pl.ds(start, size), inner, :]
        field[f, t, pl.ds(start, size), inner, :] = jnp.where(live, part, 0.0)

    for i, (f, t) in enumerate(((0, 1), (1, 1), (0, 0), (1, 0))):
        loads[i].wait()
        lax.fori_loop(0, layers // BLOCK, lambda b, c, f=f, t=t: (keep(f, t, HALO + b * BLOCK, BLOCK), c)[1], 0)

    on(velocity_down[1], velocity_down[2].wait_recv)
    on(velocity_up[1], velocity_up[2].wait_recv)
    on(has_down, sibling_low.start)
    on(has_up, sibling_high.start)
    loads[4].wait()
    on(has_far, velocity_far[1].wait_recv)
    sibling_own.wait_recv()
    sib_down, sib_up = sibling >= 2, sibling < shots - 2
    on(sib_down, sibling_low.wait_recv)
    on(sib_up, sibling_high.wait_recv)

    offset = jnp.clip(aperture_start[0] - shot + REACH, 0, REACH)
    for j in range(blocks):
        part = nearby[offset + j]
        here = pl.ds(j * brows, brows)
        alive = j * brows < live_rows
        imaging[:, here, :] = part * jnp.float32(2.0 * time_step * time_step)
        courant[:, here, :] = jnp.where(alive, part * part * jnp.float32(time_step * time_step), 0.0)

    def advance(f, t, x):
        here = pl.ds(HALO + x, BLOCK)
        now = field[f, t + 1, here, inner, :]
        high = now.astype(jnp.bfloat16)
        low = (now - high.astype(jnp.float32)).astype(jnp.bfloat16)
        both = jnp.concatenate([high, low], axis=-1).reshape(BLOCK * rows, 2 * depth)
        along_z = jnp.dot(both, depth_op[...], preferred_element_type=jnp.float32)
        total = (along_z[:, :depth] + along_z[:, depth:]).reshape(BLOCK, rows, depth)
        total = total + jnp.float32(3.0 * stencil_weights[0]) * now
        for k in range(1, HALO + 1):
            near = field[f, t + 1, pl.ds(HALO + x + k, BLOCK), inner, :]
            near = near + field[f, t + 1, pl.ds(HALO + x - k, BLOCK), inner, :]
            near = near + field[f, t + 1, here, pl.ds(PAD + k, rows), :]
            near = near + field[f, t + 1, here, pl.ds(PAD - k, rows), :]
            total = total + jnp.float32(stencil_weights[k]) * near
        own = pl.ds(x, BLOCK)
        if t == STEPS - 1:
            kept, at, row = (wave_out, adjoint_out)[f].at[0], own, 0
        else:
            kept, at, row = field.at[f, t + 2], here, PAD
        if f == 0:
            image = field[1, t + 1, here, inner, :] * total
            grad[own] = image if t == 0 else grad[own] + image
        later = 2.0 * now - field[f, t, here, inner, :] + courant[own] * total
        kept[at, pl.ds(row, PAD), :] = later[:, :PAD] + injected[f, t, own]
        kept[at, pl.ds(row + PAD, rows - PAD), :] = later[:, PAD:]

    def inside(f, t):
        lax.fori_loop(1, layers // BLOCK - 1, lambda b, c: (advance(f, t, b * BLOCK), c)[1], 0)

    def edges(f, t):
        lax.fori_loop(0, 2, lambda b, c: (advance(f, t, b * (layers - BLOCK)), c)[1], 0)

    parts = (((HALO, layers - 2 * HALO, 0),), ((0, HALO, 0), (layers - HALO, HALO, HALO)))

    def grad_copies(h):
        return (
            remote(to_sibling.at[h], from_sibling.at[h], grad_send.at[h, 0], grad_recv.at[h, 0], {"shot": sibling}),
            remote(to_far.at[h], from_far.at[h], grad_send.at[h, 1], grad_recv.at[h, 1], {"shot": far}),
            remote(to_pair.at[h, 0], from_pair.at[h, 1], grad_send.at[h, 2], grad_recv.at[h, 2], down),
            remote(to_pair.at[h, 1], from_pair.at[h, 0], grad_send.at[h, 3], grad_recv.at[h, 3], up),
        )

    grads = [grad_copies(h) for h in range(2)]
    back = 2 * REACH - offset

    def piece(h, o):
        return spread[h, back + o]

    def send_gradient(h):
        for j in range(blocks):
            here = pl.ds(j * brows, brows)
            for start, size, at in parts[h]:
                own = pl.ds(start, size)
                spread[h, REACH + j, pl.ds(at, size)] = grad[own, here, :] * imaging[own, here, :]
        toward = 1 - 2 * core
        for i, o in enumerate((0, -2, 2)):
            to_sibling[h, i] = piece(h, toward + o)
        grads[h][0].start()
        to_far[h] = piece(h, 6 * core - 3)
        on(has_far, grads[h][1].start)

    def pass_gradient(h):
        grads[h][0].wait_recv()
        to_pair[h, 0] = piece(h, -2) + from_sibling[h, 1]
        to_pair[h, 1] = piece(h, 2) + from_sibling[h, 2]
        on(has_down, grads[h][2].start)
        on(has_up, grads[h][3].start)

    def take_gradient(h):
        total = piece(h, 0) + from_sibling[h, 0]
        on(has_far, grads[h][1].wait_recv)
        on(has_up, grads[h][2].wait_recv)
        on(has_down, grads[h][3].wait_recv)
        total = total + jnp.where(has_far, from_far[h], 0.0)
        total = total + jnp.where(has_down, from_pair[h, 0], 0.0)
        total = total + jnp.where(has_up, from_pair[h, 1], 0.0)
        for start, size, at in parts[h]:
            gradient_out[pl.ds(start, size)] = total[at : at + size]

    def mask_halos(f):
        keep(f, 1, 0, HALO)
        keep(f, 1, HALO + layers, HALO)

    for t in range(STEPS - 1):
        inside(0, t)
        wait_halos(0, t)
        if t == 0:
            mask_halos(0)
        edges(0, t)
        start_halos(0, t + 1)
        inside(1, t)
        wait_halos(1, t)
        if t == 0:
            mask_halos(1)
        edges(1, t)
        start_halos(1, t + 1)

    t = STEPS - 1
    inside(0, t)
    send_gradient(0)
    inside(1, t)
    wait_halos(0, t)
    pass_gradient(0)
    edges(0, t)
    send_gradient(1)
    pass_gradient(1)
    wait_halos(1, t)
    edges(1, t)
    take_gradient(0)
    take_gradient(1)

    for f in range(2):
        for t in range(STEPS):
            for to, _, copy in halos[f][t]:
                on(to, copy.wait_send)
    for send in (velocity_far, velocity_down, velocity_up):
        on(send[0], send[-1].wait_send)
    for h in range(2):
        for to, copy in zip((None, has_far, has_down, has_up), grads[h]):
            on(to, copy.wait_send)
    sibling_own.wait_send()
    on(has_down, sibling_low.wait_send)
    on(has_up, sibling_high.wait_send)


def deliver(*refs):
    count = len(refs) // 2
    done = refs[-1]
    copies = [pltpu.make_async_copy(refs[i], refs[count + i], done.at[i]) for i in range(count)]
    for copy in copies:
        copy.start()
    for copy in copies:
        copy.wait()


def per_device(
    velocity,
    aperture_start,
    aperture_count,
    wave_prev,
    wave_now,
    adjoint_prev,
    adjoint_now,
    source_cells,
    wavelet,
    receiver_cells,
    trace,
):
    layers, brows, depth = velocity.shape
    rows = wave_now.shape[2]
    blocks = rows // brows
    block = (layers, brows, depth)
    half = (layers // 2, brows, depth)
    anywhere = pl.BlockSpec(memory_space=pl.ANY)
    f32 = jnp.float32
    out_shape = (
        jax.ShapeDtypeStruct(wave_now.shape, f32),
        jax.ShapeDtypeStruct(wave_now.shape, f32),
        jax.ShapeDtypeStruct(velocity.shape, f32),
    )
    results = pl.pallas_call(
        kernel,
        out_shape=tuple(pltpu.VMEM(leaf.shape, leaf.dtype) for leaf in out_shape),
        in_specs=[anywhere] * 11,
        out_specs=(pl.BlockSpec(memory_space=pltpu.VMEM),) * 3,
        scratch_shapes=[
            pltpu.SMEM(aperture_start.shape, jnp.int32),
            pltpu.SMEM(aperture_count.shape, jnp.int32),
            pltpu.SMEM((3, 1, source_cells.shape[1]), jnp.int32),
            pltpu.SMEM(wavelet.shape, f32),
            pltpu.SMEM((3, 1, receiver_cells.shape[1]), jnp.int32),
            pltpu.SMEM(trace.shape, f32),
            pltpu.VMEM((2, STEPS + 1, layers + 2 * HALO, rows + 2 * PAD, depth), f32),
            pltpu.VMEM((2 * REACH + 1, *block), f32),
            pltpu.VMEM((layers, rows, depth), f32),
            pltpu.VMEM((layers, rows, depth), f32),
            pltpu.VMEM((layers, rows, depth), f32),
            pltpu.VMEM((2, blocks + 2 * REACH, *half), f32),
            pltpu.VMEM((2, STEPS, layers, PAD, depth), f32),
            pltpu.VMEM((2 * depth, 2 * depth), jnp.bfloat16),
            pltpu.VMEM((2, 3, *half), f32),
            pltpu.VMEM((2, 3, *half), f32),
            pltpu.VMEM((2, *half), f32),
            pltpu.VMEM((2, *half), f32),
            pltpu.VMEM((2, 2, *half), f32),
            pltpu.VMEM((2, 2, *half), f32),
            pltpu.SemaphoreType.DMA((5,)),
            pltpu.SemaphoreType.DMA((6,)),
            pltpu.SemaphoreType.DMA((2, STEPS, 2)),
            pltpu.SemaphoreType.DMA((2, STEPS, 2)),
            pltpu.SemaphoreType.DMA((6,)),
            pltpu.SemaphoreType.DMA((6,)),
            pltpu.SemaphoreType.DMA((2, 4)),
            pltpu.SemaphoreType.DMA((2, 4)),
        ],
        compiler_params=pltpu.CompilerParams(
            collective_id=0, has_side_effects=True, vmem_limit_bytes=60 * 1024 * 1024
        ),
        name="inversion",
    )(
        velocity,
        aperture_start,
        aperture_count,
        wave_prev,
        wave_now,
        adjoint_prev,
        adjoint_now,
        jnp.transpose(source_cells, (2, 0, 1)),
        wavelet,
        jnp.transpose(receiver_cells, (2, 0, 1)),
        trace,
    )
    return pl.pallas_call(
        deliver,
        out_shape=out_shape,
        in_specs=[pl.BlockSpec(memory_space=pltpu.VMEM)] * 3,
        out_specs=(anywhere,) * 3,
        scratch_shapes=[pltpu.SemaphoreType.DMA((3,))],
        compiler_params=pltpu.CompilerParams(vmem_limit_bytes=1024 * 1024),
        name="deliver",
    )(*results)


def solution(mesh):
    fields = P("shot", "slab", None, None)
    table = P("shot", None, None)
    return jax.shard_map(
        per_device,
        mesh=mesh,
        in_specs=(P("slab", "shot", None), P("shot"), P("shot"), fields, fields, fields, fields, table, table, table, table),
        out_specs=(fields, fields, P("slab", "shot", None)),
        check_vma=False,
    )
```

```python
import functools

import jax
import jax.numpy as jnp
from jax import lax
from jax.experimental import pallas as pl
from jax.experimental.pallas import tpu as pltpu
from jax.sharding import PartitionSpec as P

MESH = pl.DeviceIdType.MESH
STEPS = 4
HALO = 4
PAD = 8
BLOCK = 4
REACH = 3

stencil_weights = (-205.0 / 72.0, 8.0 / 5.0, -1.0 / 5.0, 8.0 / 315.0, -1.0 / 560.0)
time_step = 0.09


def kernel(
    velocity,
    aperture_start_in,
    aperture_count_in,
    wave_prev,
    wave_now,
    adjoint_prev,
    adjoint_now,
    source_cells_in,
    wavelet_in,
    receiver_cells_in,
    trace_in,
    wave_out,
    adjoint_out,
    gradient_out,
    aperture_start,
    aperture_count,
    source_cells,
    wavelet,
    receiver_cells,
    trace,
    field,
    nearby_inner,
    nearby_edges,
    courant,
    imaging,
    grad,
    spread,
    injected,
    depth_op,
    to_sibling,
    from_sibling,
    to_far,
    from_far,
    to_pair,
    from_pair,
    load_sem,
    table_sem,
    halo_send,
    halo_recv,
    block_send,
    block_recv,
    grad_send,
    grad_recv,
):
    layers, rows, depth = grad.shape
    brows = velocity.shape[1]
    blocks = rows // brows
    shots, slabs = lax.axis_size("shot"), lax.axis_size("slab")
    shot, slab = lax.axis_index("shot"), lax.axis_index("slab")
    core = lax.rem(shot, 2)
    sibling = shot + 1 - 2 * core
    far = shot - 3 + 6 * core
    column = lax.rem(shot // 2, 2)
    across = shot + 2 - 4 * column
    onward, backward = shot + 4 - 8 * column, shot - 4 + 8 * column
    beside = 1 - 2 * core
    has_left, has_right = slab > 0, slab < slabs - 1
    has_far = (far >= 0) & (far < shots)
    has_down, has_up = shot >= 2, shot < shots - 2
    has_onward = (onward >= 0) & (onward < shots)
    has_backward = (backward >= 0) & (backward < shots)
    inner = pl.ds(PAD, rows)
    mine = pl.ds(HALO, layers)

    def remote(src, dst, send, recv, where):
        return pltpu.make_async_remote_copy(
            src_ref=src, dst_ref=dst, send_sem=send, recv_sem=recv, device_id=where, device_id_type=MESH
        )

    left, right = {"slab": slab - 1}, {"slab": slab + 1}
    down, up = {"shot": shot - 2}, {"shot": shot + 2}
    partners = (
        (has_left, left),
        (has_right, right),
        (has_down, down),
        (has_up, up),
        (has_onward, {"shot": onward}),
        (has_onward, {"shot": onward + beside}),
        (has_backward, {"shot": backward}),
        (has_backward, {"shot": backward + beside}),
        (None, {"shot": sibling}),
    )

    def on(condition, action):
        if condition is None:
            action()
        else:
            pl.when(condition)(action)

    nearby = (nearby_inner, nearby_edges)
    loads = [
        pltpu.make_async_copy(wave_now.at[0], field.at[0, 1, mine, inner], load_sem.at[0]),
        pltpu.make_async_copy(adjoint_now.at[0], field.at[1, 1, mine, inner], load_sem.at[1]),
        pltpu.make_async_copy(wave_prev.at[0], field.at[0, 0, mine, inner], load_sem.at[2]),
        pltpu.make_async_copy(adjoint_prev.at[0], field.at[1, 0, mine, inner], load_sem.at[3]),
        pltpu.make_async_copy(velocity.at[pl.ds(HALO, layers - 2 * HALO)], nearby_inner.at[REACH], load_sem.at[4]),
        pltpu.make_async_copy(velocity.at[pl.ds(0, HALO)], nearby_edges.at[REACH, pl.ds(0, HALO)], load_sem.at[5]),
        pltpu.make_async_copy(
            velocity.at[pl.ds(layers - HALO, HALO)], nearby_edges.at[REACH, pl.ds(HALO, HALO)], load_sem.at[6]),
    ]
    for load in loads:
        load.start()
    tables = [
        pltpu.make_async_copy(table, held, table_sem.at[i])
        for i, (table, held) in enumerate((
            (aperture_start_in, aperture_start),
            (aperture_count_in, aperture_count),
            (source_cells_in, source_cells),
            (wavelet_in, wavelet),
            (receiver_cells_in, receiver_cells),
            (trace_in, trace),
        ))
    ]
    for table in tables:
        table.start()

    def clear(edge):
        for f in range(2):
            for t in range(1, STEPS + 1):
                field[f, t, pl.ds(edge, HALO), inner, :] = jnp.zeros((HALO, rows, depth), jnp.float32)

    pl.when(jnp.logical_not(has_left))(lambda: clear(0))
    pl.when(jnp.logical_not(has_right))(lambda: clear(HALO + layers))

    barrier = pltpu.get_barrier_semaphore()
    for condition, where in partners:
        on(condition, lambda where=where: pl.semaphore_signal(barrier, inc=1, device_id=where, device_id_type=MESH))
    peers = 1
    for condition, _ in partners[:-1]:
        peers = peers + condition.astype(jnp.int32)
    pl.semaphore_wait(barrier, peers)

    def halo_copies(f, t, source):
        lo = source.at[pl.ds(0, HALO)] if t == 0 else field.at[f, t + 1, pl.ds(HALO, HALO), inner]
        hi = source.at[pl.ds(layers - HALO, HALO)] if t == 0 else field.at[f, t + 1, pl.ds(layers, HALO), inner]
        return (
            (has_left, has_right, remote(
                lo, field.at[f, t + 1, pl.ds(HALO + layers, HALO), inner],
                halo_send.at[f, t, 0], halo_recv.at[f, t, 0], left)),
            (has_right, has_left, remote(
                hi, field.at[f, t + 1, pl.ds(0, HALO), inner],
                halo_send.at[f, t, 1], halo_recv.at[f, t, 1], right)),
        )

    sources = (wave_now.at[0], adjoint_now.at[0])
    halos = [[halo_copies(f, t, sources[f]) for t in range(STEPS)] for f in range(2)]

    def start_halos(f, t):
        for to, _, copy in halos[f][t]:
            on(to, copy.start)

    def sent_halos(f, t):
        for to, _, copy in halos[f][t]:
            on(to, copy.wait_send)

    def wait_halos(f, t):
        for _, given, copy in halos[f][t]:
            on(given, copy.wait_recv)

    entry = REACH + 2 - 4 * column

    def block_copies(h):
        def send(i, source, slot, where):
            return remote(nearby[h].at[source], nearby[h].at[slot], block_send.at[h, i], block_recv.at[h, i], {"shot": where})

        return (
            (None, None, send(0, REACH, 2 * REACH - entry, across)),
            (None, None, send(1, REACH, REACH - beside, sibling)),
            (has_far, has_far, send(2, REACH, 6 * (1 - core), far)),
            (None, None, send(3, entry, entry - beside, sibling)),
            (has_onward, has_backward, send(4, entry, 2 * REACH - entry, onward)),
            (has_onward, has_backward, send(5, entry, 2 * REACH - entry - beside, onward + beside)),
        )

    block_sends = [block_copies(h) for h in range(2)]

    def send_blocks(h):
        for i in range(3):
            on(block_sends[h][i][0], block_sends[h][i][2].start)

    def forward_blocks(h):
        block_sends[h][0][2].wait_recv()
        for i in (4, 5, 3):
            on(block_sends[h][i][0], block_sends[h][i][2].start)

    def wait_blocks(h):
        for i in range(1, 6):
            on(block_sends[h][i][1], block_sends[h][i][2].wait_recv)

    for load in loads[4:]:
        load.wait()
    send_blocks(1)
    start_halos(0, 0)
    send_blocks(0)

    def clear_rows(i, carry):
        for f in range(2):
            for t in range(1, STEPS + 1):
                field[f, t, HALO + i, pl.ds(0, PAD), :] = jnp.zeros((PAD, depth), jnp.float32)
                field[f, t, HALO + i, pl.ds(PAD + rows, PAD), :] = jnp.zeros((PAD, depth), jnp.float32)
        return carry

    lax.fori_loop(0, layers, clear_rows, 0)
    for h in range(2):
        for j in range(REACH):
            spread[h, j] = jnp.zeros(spread.shape[2:], jnp.float32)
            spread[h, REACH + blocks + j] = jnp.zeros(spread.shape[2:], jnp.float32)

    apart = jnp.abs(
        lax.broadcasted_iota(jnp.int32, (depth, depth), 0) - lax.broadcasted_iota(jnp.int32, (depth, depth), 1)
    )
    operator = jnp.zeros((depth, depth), jnp.float32)
    for k in range(1, HALO + 1):
        operator = jnp.where(apart == k, jnp.float32(stencil_weights[k]), operator)
    op_high = operator.astype(jnp.bfloat16)
    op_low = (operator - op_high.astype(jnp.float32)).astype(jnp.bfloat16)
    for half in range(2):
        depth_op[pl.ds(half * depth, depth), pl.ds(0, depth)] = op_high
        depth_op[pl.ds(half * depth, depth), pl.ds(depth, depth)] = op_low

    for table in tables:
        table.wait()
    live_rows = aperture_count[0] * brows
    at_row = lax.broadcasted_iota(jnp.int32, (1, rows, depth), 1)
    live = at_row < live_rows

    def keep(f, t, start, size):
        part = field[f, t, pl.ds(start, size), inner, :]
        field[f, t, pl.ds(start, size), inner, :] = jnp.where(live, part, 0.0)

    for i, (f, t) in enumerate(((0, 1), (1, 1), (0, 0), (1, 0))):
        loads[i].wait()
        lax.fori_loop(0, layers // BLOCK, lambda b, c, f=f, t=t: (keep(f, t, HALO + b * BLOCK, BLOCK), c)[1], 0)

    forward_blocks(1)
    sent_halos(0, 0)
    start_halos(1, 0)

    at_y = lax.broadcasted_iota(jnp.int32, (PAD, depth), 0)
    at_z = lax.broadcasted_iota(jnp.int32, (PAD, depth), 1)
    first = slab * layers
    for f, (cells, amps) in enumerate(((source_cells, wavelet), (receiver_cells, trace))):
        count = cells.shape[-1]

        def inject(x, carry, f=f, cells=cells, amps=amps, count=count):
            sums = [jnp.zeros((PAD, depth), jnp.float32)] * STEPS
            for s in range(count):
                hit = (at_y == cells[1, 0, s]) & (at_z == cells[2, 0, s])
                here = cells[0, 0, s] == first + x
                for t in range(STEPS):
                    amp = jnp.where(here, amps[0, t, s], 0.0)
                    sums[t] = sums[t] + jnp.where(hit, amp, 0.0)
            for t in range(STEPS):
                injected[f, t, x] = sums[t]
            return carry

        lax.fori_loop(0, layers, inject, 0)

    forward_blocks(0)

    offset = jnp.clip(aperture_start[0] - shot + REACH, 0, REACH)
    parts = (((HALO, layers - 2 * HALO, 0),), ((0, HALO, 0), (layers - HALO, HALO, HALO)))

    def lay_window(h):
        wait_blocks(h)
        for j in range(blocks):
            here = pl.ds(j * brows, brows)
            alive = j * brows < live_rows
            for start, size, at in parts[h]:
                part = nearby[h][offset + j, pl.ds(at, size)]
                imaging[pl.ds(start, size), here, :] = part * jnp.float32(2.0 * time_step * time_step)
                courant[pl.ds(start, size), here, :] = jnp.where(
                    alive, part * part * jnp.float32(time_step * time_step), 0.0
                )

    def advance(f, t, x):
        here = pl.ds(HALO + x, BLOCK)
        now = field[f, t + 1, here, inner, :]
        high = now.astype(jnp.bfloat16)
        low = (now - high.astype(jnp.float32)).astype(jnp.bfloat16)
        both = jnp.concatenate([high, low], axis=-1).reshape(BLOCK * rows, 2 * depth)
        along_z = jnp.dot(both, depth_op[...], preferred_element_type=jnp.float32)
        total = (along_z[:, :depth] + along_z[:, depth:]).reshape(BLOCK, rows, depth)
        total = total + jnp.float32(3.0 * stencil_weights[0]) * now
        for k in range(1, HALO + 1):
            near = field[f, t + 1, pl.ds(HALO + x + k, BLOCK), inner, :]
            near = near + field[f, t + 1, pl.ds(HALO + x - k, BLOCK), inner, :]
            near = near + field[f, t + 1, here, pl.ds(PAD + k, rows), :]
            near = near + field[f, t + 1, here, pl.ds(PAD - k, rows), :]
            total = total + jnp.float32(stencil_weights[k]) * near
        own = pl.ds(x, BLOCK)
        if t == STEPS - 1:
            kept, at, row = (wave_out, adjoint_out)[f].at[0], own, 0
        else:
            kept, at, row = field.at[f, t + 2], here, PAD
        if f == 0:
            image = field[1, t + 1, here, inner, :] * total
            grad[own] = image if t == 0 else grad[own] + image
        later = 2.0 * now - field[f, t, here, inner, :] + courant[own] * total
        kept[at, pl.ds(row, PAD), :] = later[:, :PAD] + injected[f, t, own]
        kept[at, pl.ds(row + PAD, rows - PAD), :] = later[:, PAD:]

    def inside(f, t):
        lax.fori_loop(1, layers // BLOCK - 1, lambda b, c: (advance(f, t, b * BLOCK), c)[1], 0)

    def edges(f, t):
        lax.fori_loop(0, 2, lambda b, c: (advance(f, t, b * (layers - BLOCK)), c)[1], 0)

    def grad_copies(h):
        return (
            remote(to_sibling.at[h], from_sibling.at[h], grad_send.at[h, 0], grad_recv.at[h, 0], {"shot": sibling}),
            remote(to_far.at[h], from_far.at[h], grad_send.at[h, 1], grad_recv.at[h, 1], {"shot": far}),
            remote(to_pair.at[h, 0], from_pair.at[h, 1], grad_send.at[h, 2], grad_recv.at[h, 2], down),
            remote(to_pair.at[h, 1], from_pair.at[h, 0], grad_send.at[h, 3], grad_recv.at[h, 3], up),
        )

    grads = [grad_copies(h) for h in range(2)]
    back = 2 * REACH - offset

    def piece(h, o):
        return spread[h, back + o]

    def send_gradient(h):
        for j in range(blocks):
            here = pl.ds(j * brows, brows)
            for start, size, at in parts[h]:
                own = pl.ds(start, size)
                spread[h, REACH + j, pl.ds(at, size)] = grad[own, here, :] * imaging[own, here, :]
        toward = 1 - 2 * core
        for i, o in enumerate((0, -2, 2)):
            to_sibling[h, i] = piece(h, toward + o)
        grads[h][0].start()
        to_far[h] = piece(h, 6 * core - 3)
        on(has_far, grads[h][1].start)

    def pass_gradient(h):
        grads[h][0].wait_recv()
        to_pair[h, 0] = piece(h, -2) + from_sibling[h, 1]
        to_pair[h, 1] = piece(h, 2) + from_sibling[h, 2]
        on(has_down, grads[h][2].start)
        on(has_up, grads[h][3].start)

    def take_gradient(h):
        total = piece(h, 0) + from_sibling[h, 0]
        on(has_far, grads[h][1].wait_recv)
        on(has_up, grads[h][2].wait_recv)
        on(has_down, grads[h][3].wait_recv)
        total = total + jnp.where(has_far, from_far[h], 0.0)
        total = total + jnp.where(has_down, from_pair[h, 0], 0.0)
        total = total + jnp.where(has_up, from_pair[h, 1], 0.0)
        for start, size, at in parts[h]:
            gradient_out[pl.ds(start, size)] = total[at : at + size]

    def mask_halos(f):
        keep(f, 1, 0, HALO)
        keep(f, 1, HALO + layers, HALO)

    lay_window(1)
    for f in range(2):
        wait_halos(f, 0)
        mask_halos(f)
        edges(f, 0)
        if f:
            sent_halos(0, 1)
        else:
            sent_halos(1, 0)
        start_halos(f, 1)
    lay_window(0)
    inside(0, 0)
    inside(1, 0)

    for t in range(1, STEPS - 1):
        for f in range(2):
            inside(f, t)
            wait_halos(f, t)
            edges(f, t)
            sent_halos(1 - f, t + f)
            start_halos(f, t + 1)

    t = STEPS - 1
    inside(0, t)
    send_gradient(0)
    inside(1, t)
    wait_halos(0, t)
    pass_gradient(0)
    edges(0, t)
    send_gradient(1)
    pass_gradient(1)
    wait_halos(1, t)
    edges(1, t)
    take_gradient(0)
    take_gradient(1)

    sent_halos(1, STEPS - 1)
    for h in range(2):
        for to, _, copy in block_sends[h]:
            on(to, copy.wait_send)
    for h in range(2):
        for to, copy in zip((None, has_far, has_down, has_up), grads[h]):
            on(to, copy.wait_send)


def deliver(*refs):
    count = len(refs) // 2
    done = refs[-1]
    copies = [pltpu.make_async_copy(refs[i], refs[count + i], done.at[i]) for i in range(count)]
    for copy in copies:
        copy.start()
    for copy in copies:
        copy.wait()


def per_device(
    velocity,
    aperture_start,
    aperture_count,
    wave_prev,
    wave_now,
    adjoint_prev,
    adjoint_now,
    source_cells,
    wavelet,
    receiver_cells,
    trace,
):
    layers, brows, depth = velocity.shape
    rows = wave_now.shape[2]
    blocks = rows // brows
    block = (layers, brows, depth)
    half = (layers // 2, brows, depth)
    anywhere = pl.BlockSpec(memory_space=pl.ANY)
    f32 = jnp.float32
    out_shape = (
        jax.ShapeDtypeStruct(wave_now.shape, f32),
        jax.ShapeDtypeStruct(wave_now.shape, f32),
        jax.ShapeDtypeStruct(velocity.shape, f32),
    )
    results = pl.pallas_call(
        kernel,
        out_shape=tuple(pltpu.VMEM(leaf.shape, leaf.dtype) for leaf in out_shape),
        in_specs=[anywhere] * 11,
        out_specs=(pl.BlockSpec(memory_space=pltpu.VMEM),) * 3,
        scratch_shapes=[
            pltpu.SMEM(aperture_start.shape, jnp.int32),
            pltpu.SMEM(aperture_count.shape, jnp.int32),
            pltpu.SMEM((3, 1, source_cells.shape[1]), jnp.int32),
            pltpu.SMEM(wavelet.shape, f32),
            pltpu.SMEM((3, 1, receiver_cells.shape[1]), jnp.int32),
            pltpu.SMEM(trace.shape, f32),
            pltpu.VMEM((2, STEPS + 1, layers + 2 * HALO, rows + 2 * PAD, depth), f32),
            pltpu.VMEM((2 * REACH + 1, *half), f32),
            pltpu.VMEM((2 * REACH + 1, *half), f32),
            pltpu.VMEM((layers, rows, depth), f32),
            pltpu.VMEM((layers, rows, depth), f32),
            pltpu.VMEM((layers, rows, depth), f32),
            pltpu.VMEM((2, blocks + 2 * REACH, *half), f32),
            pltpu.VMEM((2, STEPS, layers, PAD, depth), f32),
            pltpu.VMEM((2 * depth, 2 * depth), jnp.bfloat16),
            pltpu.VMEM((2, 3, *half), f32),
            pltpu.VMEM((2, 3, *half), f32),
            pltpu.VMEM((2, *half), f32),
            pltpu.VMEM((2, *half), f32),
            pltpu.VMEM((2, 2, *half), f32),
            pltpu.VMEM((2, 2, *half), f32),
            pltpu.SemaphoreType.DMA((7,)),
            pltpu.SemaphoreType.DMA((6,)),
            pltpu.SemaphoreType.DMA((2, STEPS, 2)),
            pltpu.SemaphoreType.DMA((2, STEPS, 2)),
            pltpu.SemaphoreType.DMA((2, 6)),
            pltpu.SemaphoreType.DMA((2, 6)),
            pltpu.SemaphoreType.DMA((2, 4)),
            pltpu.SemaphoreType.DMA((2, 4)),
        ],
        compiler_params=pltpu.CompilerParams(
            collective_id=0, has_side_effects=True, vmem_limit_bytes=60 * 1024 * 1024
        ),
        name="inversion",
    )(
        velocity,
        aperture_start,
        aperture_count,
        wave_prev,
        wave_now,
        adjoint_prev,
        adjoint_now,
        jnp.transpose(source_cells, (2, 0, 1)),
        wavelet,
        jnp.transpose(receiver_cells, (2, 0, 1)),
        trace,
    )
    return pl.pallas_call(
        deliver,
        out_shape=out_shape,
        in_specs=[pl.BlockSpec(memory_space=pltpu.VMEM)] * 3,
        out_specs=(anywhere,) * 3,
        scratch_shapes=[pltpu.SemaphoreType.DMA((3,))],
        compiler_params=pltpu.CompilerParams(vmem_limit_bytes=1024 * 1024),
        name="deliver",
    )(*results)


def solution(mesh):
    fields = P("shot", "slab", None, None)
    table = P("shot", None, None)
    return jax.shard_map(
        per_device,
        mesh=mesh,
        in_specs=(P("slab", "shot", None), P("shot"), P("shot"), fields, fields, fields, fields, table, table, table, table),
        out_specs=(fields, fields, P("slab", "shot", None)),
        check_vma=False,
    )
```

```python
import functools

import jax
import jax.numpy as jnp
from jax import lax
from jax.experimental import pallas as pl
from jax.experimental.pallas import tpu as pltpu
from jax.sharding import PartitionSpec as P

MESH = pl.DeviceIdType.MESH
STEPS = 4
HALO = 4
PAD = 8
BLOCK = 4
REACH = 3

stencil_weights = (-205.0 / 72.0, 8.0 / 5.0, -1.0 / 5.0, 8.0 / 315.0, -1.0 / 560.0)
time_step = 0.09


def kernel(
    velocity,
    aperture_start_in,
    aperture_count_in,
    wave_prev,
    wave_now,
    adjoint_prev,
    adjoint_now,
    source_cells_in,
    wavelet_in,
    receiver_cells_in,
    trace_in,
    wave_out,
    adjoint_out,
    gradient_out,
    aperture_start,
    aperture_count,
    source_cells,
    wavelet,
    receiver_cells,
    trace,
    field,
    nearby_inner,
    nearby_edges,
    courant,
    imaging,
    grad,
    spread,
    injected,
    depth_op,
    to_sibling,
    from_sibling,
    to_far,
    from_far,
    to_pair,
    from_pair,
    load_sem,
    table_sem,
    halo_send,
    halo_recv,
    block_send,
    block_recv,
    grad_send,
    grad_recv,
):
    layers, rows, depth = grad.shape
    brows = velocity.shape[1]
    blocks = rows // brows
    shots, slabs = lax.axis_size("shot"), lax.axis_size("slab")
    shot, slab = lax.axis_index("shot"), lax.axis_index("slab")
    core = lax.rem(shot, 2)
    sibling = shot + 1 - 2 * core
    far = shot - 3 + 6 * core
    column = lax.rem(shot // 2, 2)
    across = shot + 2 - 4 * column
    onward, backward = shot + 4 - 8 * column, shot - 4 + 8 * column
    beside = 1 - 2 * core
    has_left, has_right = slab > 0, slab < slabs - 1
    has_far = (far >= 0) & (far < shots)
    has_down, has_up = shot >= 2, shot < shots - 2
    has_onward = (onward >= 0) & (onward < shots)
    has_backward = (backward >= 0) & (backward < shots)
    inner = pl.ds(PAD, rows)
    mine = pl.ds(HALO, layers)

    def remote(src, dst, send, recv, where):
        return pltpu.make_async_remote_copy(
            src_ref=src, dst_ref=dst, send_sem=send, recv_sem=recv, device_id=where, device_id_type=MESH
        )

    left, right = {"slab": slab - 1}, {"slab": slab + 1}
    down, up = {"shot": shot - 2}, {"shot": shot + 2}
    partners = (
        (has_left, left),
        (has_right, right),
        (has_down, down),
        (has_up, up),
        (has_onward, {"shot": onward}),
        (has_onward, {"shot": onward + beside}),
        (has_backward, {"shot": backward}),
        (has_backward, {"shot": backward + beside}),
        (None, {"shot": sibling}),
    )

    def on(condition, action):
        if condition is None:
            action()
        else:
            pl.when(condition)(action)

    nearby = (nearby_inner, nearby_edges)
    loads = [
        pltpu.make_async_copy(wave_now.at[0], field.at[0, 1, mine, inner], load_sem.at[0]),
        pltpu.make_async_copy(adjoint_now.at[0], field.at[1, 1, mine, inner], load_sem.at[1]),
        pltpu.make_async_copy(wave_prev.at[0], field.at[0, 0, mine, inner], load_sem.at[2]),
        pltpu.make_async_copy(adjoint_prev.at[0], field.at[1, 0, mine, inner], load_sem.at[3]),
        pltpu.make_async_copy(velocity.at[pl.ds(HALO, layers - 2 * HALO)], nearby_inner.at[REACH], load_sem.at[4]),
        pltpu.make_async_copy(velocity.at[pl.ds(0, HALO)], nearby_edges.at[REACH, pl.ds(0, HALO)], load_sem.at[5]),
        pltpu.make_async_copy(
            velocity.at[pl.ds(layers - HALO, HALO)], nearby_edges.at[REACH, pl.ds(HALO, HALO)], load_sem.at[6]),
    ]
    for load in loads:
        load.start()
    tables = [
        pltpu.make_async_copy(table, held, table_sem.at[i])
        for i, (table, held) in enumerate((
            (aperture_start_in, aperture_start),
            (aperture_count_in, aperture_count),
            (source_cells_in, source_cells),
            (wavelet_in, wavelet),
            (receiver_cells_in, receiver_cells),
            (trace_in, trace),
        ))
    ]
    for table in tables:
        table.start()

    def clear(edge):
        for f in range(2):
            for t in range(1, STEPS + 1):
                field[f, t, pl.ds(edge, HALO), inner, :] = jnp.zeros((HALO, rows, depth), jnp.float32)

    pl.when(jnp.logical_not(has_left))(lambda: clear(0))
    pl.when(jnp.logical_not(has_right))(lambda: clear(HALO + layers))

    barrier = pltpu.get_barrier_semaphore()
    for condition, where in partners:
        on(condition, lambda where=where: pl.semaphore_signal(barrier, inc=1, device_id=where, device_id_type=MESH))
    peers = 1
    for condition, _ in partners[:-1]:
        peers = peers + condition.astype(jnp.int32)
    pl.semaphore_wait(barrier, peers)

    def halo_copies(f, t, source):
        lo = source.at[pl.ds(0, HALO)] if t == 0 else field.at[f, t + 1, pl.ds(HALO, HALO), inner]
        hi = source.at[pl.ds(layers - HALO, HALO)] if t == 0 else field.at[f, t + 1, pl.ds(layers, HALO), inner]
        return (
            (has_left, has_right, remote(
                lo, field.at[f, t + 1, pl.ds(HALO + layers, HALO), inner],
                halo_send.at[f, t, 0], halo_recv.at[f, t, 0], left)),
            (has_right, has_left, remote(
                hi, field.at[f, t + 1, pl.ds(0, HALO), inner],
                halo_send.at[f, t, 1], halo_recv.at[f, t, 1], right)),
        )

    sources = (wave_now.at[0], adjoint_now.at[0])
    halos = [[halo_copies(f, t, sources[f]) for t in range(STEPS)] for f in range(2)]

    def start_halos(f, t):
        for to, _, copy in halos[f][t]:
            on(to, copy.start)

    def sent_halos(f, t):
        for to, _, copy in halos[f][t]:
            on(to, copy.wait_send)

    def wait_halos(f, t):
        for _, given, copy in halos[f][t]:
            on(given, copy.wait_recv)

    entry = REACH + 2 - 4 * column

    def block_copies(h):
        def send(i, source, slot, where):
            return remote(nearby[h].at[source], nearby[h].at[slot], block_send.at[h, i], block_recv.at[h, i], {"shot": where})

        return (
            (None, None, send(0, REACH, 2 * REACH - entry, across)),
            (None, None, send(1, REACH, REACH - beside, sibling)),
            (has_far, has_far, send(2, REACH, 6 * (1 - core), far)),
            (None, None, send(3, entry, entry - beside, sibling)),
            (has_onward, has_backward, send(4, entry, 2 * REACH - entry, onward)),
            (has_onward, has_backward, send(5, entry, 2 * REACH - entry - beside, onward + beside)),
        )

    block_sends = [block_copies(h) for h in range(2)]

    def send_blocks(h):
        for i in range(3):
            on(block_sends[h][i][0], block_sends[h][i][2].start)

    def forward_blocks(h):
        block_sends[h][0][2].wait_recv()
        for i in (4, 5, 3):
            on(block_sends[h][i][0], block_sends[h][i][2].start)

    def wait_blocks(h):
        for i in range(1, 6):
            on(block_sends[h][i][1], block_sends[h][i][2].wait_recv)

    for load in loads[4:]:
        load.wait()
    send_blocks(1)
    start_halos(0, 0)

    def clear_rows(i, carry):
        for f in range(2):
            for t in range(1, STEPS + 1):
                field[f, t, HALO + i, pl.ds(0, PAD), :] = jnp.zeros((PAD, depth), jnp.float32)
                field[f, t, HALO + i, pl.ds(PAD + rows, PAD), :] = jnp.zeros((PAD, depth), jnp.float32)
        return carry

    lax.fori_loop(0, layers, clear_rows, 0)
    for h in range(2):
        for j in range(REACH):
            spread[h, j] = jnp.zeros(spread.shape[2:], jnp.float32)
            spread[h, REACH + blocks + j] = jnp.zeros(spread.shape[2:], jnp.float32)

    apart = jnp.abs(
        lax.broadcasted_iota(jnp.int32, (depth, depth), 0) - lax.broadcasted_iota(jnp.int32, (depth, depth), 1)
    )
    operator = jnp.zeros((depth, depth), jnp.float32)
    for k in range(1, HALO + 1):
        operator = jnp.where(apart == k, jnp.float32(stencil_weights[k]), operator)
    op_high = operator.astype(jnp.bfloat16)
    op_low = (operator - op_high.astype(jnp.float32)).astype(jnp.bfloat16)
    for half in range(2):
        depth_op[pl.ds(half * depth, depth), pl.ds(0, depth)] = op_high
        depth_op[pl.ds(half * depth, depth), pl.ds(depth, depth)] = op_low

    forward_blocks(1)

    for table in tables:
        table.wait()
    live_rows = aperture_count[0] * brows
    at_row = lax.broadcasted_iota(jnp.int32, (1, rows, depth), 1)
    live = at_row < live_rows

    def keep(f, t, start, size):
        part = field[f, t, pl.ds(start, size), inner, :]
        field[f, t, pl.ds(start, size), inner, :] = jnp.where(live, part, 0.0)

    for i, (f, t) in enumerate(((0, 1), (1, 1), (0, 0), (1, 0))):
        loads[i].wait()
        lax.fori_loop(0, layers // BLOCK, lambda b, c, f=f, t=t: (keep(f, t, HALO + b * BLOCK, BLOCK), c)[1], 0)

    send_blocks(0)
    sent_halos(0, 0)
    start_halos(1, 0)

    at_y = lax.broadcasted_iota(jnp.int32, (PAD, depth), 0)
    at_z = lax.broadcasted_iota(jnp.int32, (PAD, depth), 1)
    first = slab * layers
    for f, (cells, amps) in enumerate(((source_cells, wavelet), (receiver_cells, trace))):
        count = cells.shape[-1]

        def inject(x, carry, f=f, cells=cells, amps=amps, count=count):
            sums = [jnp.zeros((PAD, depth), jnp.float32)] * STEPS
            for s in range(count):
                hit = (at_y == cells[1, 0, s]) & (at_z == cells[2, 0, s])
                here = cells[0, 0, s] == first + x
                for t in range(STEPS):
                    amp = jnp.where(here, amps[0, t, s], 0.0)
                    sums[t] = sums[t] + jnp.where(hit, amp, 0.0)
            for t in range(STEPS):
                injected[f, t, x] = sums[t]
            return carry

        lax.fori_loop(0, layers, inject, 0)

    forward_blocks(0)

    offset = jnp.clip(aperture_start[0] - shot + REACH, 0, REACH)
    parts = (((HALO, layers - 2 * HALO, 0),), ((0, HALO, 0), (layers - HALO, HALO, HALO)))

    def lay_window(h):
        wait_blocks(h)
        for j in range(blocks):
            here = pl.ds(j * brows, brows)
            alive = j * brows < live_rows
            for start, size, at in parts[h]:
                part = nearby[h][offset + j, pl.ds(at, size)]
                imaging[pl.ds(start, size), here, :] = part * jnp.float32(2.0 * time_step * time_step)
                courant[pl.ds(start, size), here, :] = jnp.where(
                    alive, part * part * jnp.float32(time_step * time_step), 0.0
                )

    def advance(f, t, x):
        here = pl.ds(HALO + x, BLOCK)
        now = field[f, t + 1, here, inner, :]
        high = now.astype(jnp.bfloat16)
        low = (now - high.astype(jnp.float32)).astype(jnp.bfloat16)
        both = jnp.concatenate([high, low], axis=-1).reshape(BLOCK * rows, 2 * depth)
        along_z = jnp.dot(both, depth_op[...], preferred_element_type=jnp.float32)
        total = (along_z[:, :depth] + along_z[:, depth:]).reshape(BLOCK, rows, depth)
        total = total + jnp.float32(3.0 * stencil_weights[0]) * now
        for k in range(1, HALO + 1):
            near = field[f, t + 1, pl.ds(HALO + x + k, BLOCK), inner, :]
            near = near + field[f, t + 1, pl.ds(HALO + x - k, BLOCK), inner, :]
            near = near + field[f, t + 1, here, pl.ds(PAD + k, rows), :]
            near = near + field[f, t + 1, here, pl.ds(PAD - k, rows), :]
            total = total + jnp.float32(stencil_weights[k]) * near
        own = pl.ds(x, BLOCK)
        if t == STEPS - 1:
            kept, at, row = (wave_out, adjoint_out)[f].at[0], own, 0
        else:
            kept, at, row = field.at[f, t + 2], here, PAD
        if f == 0:
            image = field[1, t + 1, here, inner, :] * total
            grad[own] = image if t == 0 else grad[own] + image
        later = 2.0 * now - field[f, t, here, inner, :] + courant[own] * total
        kept[at, pl.ds(row, PAD), :] = later[:, :PAD] + injected[f, t, own]
        kept[at, pl.ds(row + PAD, rows - PAD), :] = later[:, PAD:]

    def inside(f, t):
        lax.fori_loop(1, layers // BLOCK - 1, lambda b, c: (advance(f, t, b * BLOCK), c)[1], 0)

    def edges(f, t):
        lax.fori_loop(0, 2, lambda b, c: (advance(f, t, b * (layers - BLOCK)), c)[1], 0)

    def grad_copies(h):
        return (
            remote(to_sibling.at[h], from_sibling.at[h], grad_send.at[h, 0], grad_recv.at[h, 0], {"shot": sibling}),
            remote(to_far.at[h], from_far.at[h], grad_send.at[h, 1], grad_recv.at[h, 1], {"shot": far}),
            remote(to_pair.at[h, 0], from_pair.at[h, 1], grad_send.at[h, 2], grad_recv.at[h, 2], down),
            remote(to_pair.at[h, 1], from_pair.at[h, 0], grad_send.at[h, 3], grad_recv.at[h, 3], up),
        )

    grads = [grad_copies(h) for h in range(2)]
    back = 2 * REACH - offset

    def piece(h, o):
        return spread[h, back + o]

    def send_gradient(h):
        for j in range(blocks):
            here = pl.ds(j * brows, brows)
            for start, size, at in parts[h]:
                own = pl.ds(start, size)
                spread[h, REACH + j, pl.ds(at, size)] = grad[own, here, :] * imaging[own, here, :]
        toward = 1 - 2 * core
        for i, o in enumerate((0, -2, 2)):
            to_sibling[h, i] = piece(h, toward + o)
        grads[h][0].start()
        to_far[h] = piece(h, 6 * core - 3)
        on(has_far, grads[h][1].start)

    def pass_gradient(h):
        grads[h][0].wait_recv()
        to_pair[h, 0] = piece(h, -2) + from_sibling[h, 1]
        to_pair[h, 1] = piece(h, 2) + from_sibling[h, 2]
        on(has_down, grads[h][2].start)
        on(has_up, grads[h][3].start)

    def take_gradient(h):
        total = piece(h, 0) + from_sibling[h, 0]
        on(has_far, grads[h][1].wait_recv)
        on(has_up, grads[h][2].wait_recv)
        on(has_down, grads[h][3].wait_recv)
        total = total + jnp.where(has_far, from_far[h], 0.0)
        total = total + jnp.where(has_down, from_pair[h, 0], 0.0)
        total = total + jnp.where(has_up, from_pair[h, 1], 0.0)
        for start, size, at in parts[h]:
            gradient_out[pl.ds(start, size)] = total[at : at + size]

    def mask_halos(f):
        keep(f, 1, 0, HALO)
        keep(f, 1, HALO + layers, HALO)

    lay_window(1)
    for f in range(2):
        wait_halos(f, 0)
        mask_halos(f)
        edges(f, 0)
        if f:
            sent_halos(0, 1)
        start_halos(f, 1)
    lay_window(0)
    inside(0, 0)
    inside(1, 0)

    for t in range(1, STEPS - 1):
        for f in range(2):
            inside(f, t)
            wait_halos(f, t)
            edges(f, t)
            if f:
                sent_halos(0, t + 1)
            start_halos(f, t + 1)

    t = STEPS - 1
    inside(0, t)
    send_gradient(0)
    inside(1, t)
    wait_halos(0, t)
    pass_gradient(0)
    edges(0, t)
    send_gradient(1)
    pass_gradient(1)
    wait_halos(1, t)
    edges(1, t)
    take_gradient(0)
    take_gradient(1)

    for t in range(STEPS):
        sent_halos(1, t)
    for h in range(2):
        for to, _, copy in block_sends[h]:
            on(to, copy.wait_send)
    for h in range(2):
        for to, copy in zip((None, has_far, has_down, has_up), grads[h]):
            on(to, copy.wait_send)


def deliver(*refs):
    count = len(refs) // 2
    done = refs[-1]
    copies = [pltpu.make_async_copy(refs[i], refs[count + i], done.at[i]) for i in range(count)]
    for copy in copies:
        copy.start()
    for copy in copies:
        copy.wait()


def per_device(
    velocity,
    aperture_start,
    aperture_count,
    wave_prev,
    wave_now,
    adjoint_prev,
    adjoint_now,
    source_cells,
    wavelet,
    receiver_cells,
    trace,
):
    layers, brows, depth = velocity.shape
    rows = wave_now.shape[2]
    blocks = rows // brows
    block = (layers, brows, depth)
    half = (layers // 2, brows, depth)
    anywhere = pl.BlockSpec(memory_space=pl.ANY)
    f32 = jnp.float32
    out_shape = (
        jax.ShapeDtypeStruct(wave_now.shape, f32),
        jax.ShapeDtypeStruct(wave_now.shape, f32),
        jax.ShapeDtypeStruct(velocity.shape, f32),
    )
    results = pl.pallas_call(
        kernel,
        out_shape=tuple(pltpu.VMEM(leaf.shape, leaf.dtype) for leaf in out_shape),
        in_specs=[anywhere] * 11,
        out_specs=(pl.BlockSpec(memory_space=pltpu.VMEM),) * 3,
        scratch_shapes=[
            pltpu.SMEM(aperture_start.shape, jnp.int32),
            pltpu.SMEM(aperture_count.shape, jnp.int32),
            pltpu.SMEM((3, 1, source_cells.shape[1]), jnp.int32),
            pltpu.SMEM(wavelet.shape, f32),
            pltpu.SMEM((3, 1, receiver_cells.shape[1]), jnp.int32),
            pltpu.SMEM(trace.shape, f32),
            pltpu.VMEM((2, STEPS + 1, layers + 2 * HALO, rows + 2 * PAD, depth), f32),
            pltpu.VMEM((2 * REACH + 1, *half), f32),
            pltpu.VMEM((2 * REACH + 1, *half), f32),
            pltpu.VMEM((layers, rows, depth), f32),
            pltpu.VMEM((layers, rows, depth), f32),
            pltpu.VMEM((layers, rows, depth), f32),
            pltpu.VMEM((2, blocks + 2 * REACH, *half), f32),
            pltpu.VMEM((2, STEPS, layers, PAD, depth), f32),
            pltpu.VMEM((2 * depth, 2 * depth), jnp.bfloat16),
            pltpu.VMEM((2, 3, *half), f32),
            pltpu.VMEM((2, 3, *half), f32),
            pltpu.VMEM((2, *half), f32),
            pltpu.VMEM((2, *half), f32),
            pltpu.VMEM((2, 2, *half), f32),
            pltpu.VMEM((2, 2, *half), f32),
            pltpu.SemaphoreType.DMA((7,)),
            pltpu.SemaphoreType.DMA((6,)),
            pltpu.SemaphoreType.DMA((2, STEPS, 2)),
            pltpu.SemaphoreType.DMA((2, STEPS, 2)),
            pltpu.SemaphoreType.DMA((2, 6)),
            pltpu.SemaphoreType.DMA((2, 6)),
            pltpu.SemaphoreType.DMA((2, 4)),
            pltpu.SemaphoreType.DMA((2, 4)),
        ],
        compiler_params=pltpu.CompilerParams(
            collective_id=0, has_side_effects=True, vmem_limit_bytes=60 * 1024 * 1024
        ),
        name="inversion",
    )(
        velocity,
        aperture_start,
        aperture_count,
        wave_prev,
        wave_now,
        adjoint_prev,
        adjoint_now,
        jnp.transpose(source_cells, (2, 0, 1)),
        wavelet,
        jnp.transpose(receiver_cells, (2, 0, 1)),
        trace,
    )
    return pl.pallas_call(
        deliver,
        out_shape=out_shape,
        in_specs=[pl.BlockSpec(memory_space=pltpu.VMEM)] * 3,
        out_specs=(anywhere,) * 3,
        scratch_shapes=[pltpu.SemaphoreType.DMA((3,))],
        compiler_params=pltpu.CompilerParams(vmem_limit_bytes=1024 * 1024),
        name="deliver",
    )(*results)


def solution(mesh):
    fields = P("shot", "slab", None, None)
    table = P("shot", None, None)
    return jax.shard_map(
        per_device,
        mesh=mesh,
        in_specs=(P("slab", "shot", None), P("shot"), P("shot"), fields, fields, fields, fields, table, table, table, table),
        out_specs=(fields, fields, P("slab", "shot", None)),
        check_vma=False,
    )
```

```python
import functools

import jax
import jax.numpy as jnp
from jax import lax
from jax.experimental import pallas as pl
from jax.experimental.pallas import tpu as pltpu
from jax.sharding import PartitionSpec as P

MESH = pl.DeviceIdType.MESH
STEPS = 4
HALO = 4
PAD = 8
BLOCK = 4
REACH = 3

stencil_weights = (-205.0 / 72.0, 8.0 / 5.0, -1.0 / 5.0, 8.0 / 315.0, -1.0 / 560.0)
time_step = 0.09


def kernel(
    velocity,
    aperture_start_in,
    aperture_count_in,
    wave_prev,
    wave_now,
    adjoint_prev,
    adjoint_now,
    source_cells_in,
    wavelet_in,
    receiver_cells_in,
    trace_in,
    wave_out,
    adjoint_out,
    gradient_out,
    aperture_start,
    aperture_count,
    source_cells,
    wavelet,
    receiver_cells,
    trace,
    field,
    nearby_inner,
    nearby_edges,
    courant,
    imaging,
    grad,
    spread,
    injected,
    depth_op,
    to_sibling,
    from_sibling,
    to_far,
    from_far,
    to_pair,
    from_pair,
    load_sem,
    table_sem,
    halo_send,
    halo_recv,
    block_send,
    block_recv,
    grad_send,
    grad_recv,
):
    layers, rows, depth = grad.shape
    brows = velocity.shape[1]
    blocks = rows // brows
    shots, slabs = lax.axis_size("shot"), lax.axis_size("slab")
    shot, slab = lax.axis_index("shot"), lax.axis_index("slab")
    core = lax.rem(shot, 2)
    sibling = shot + 1 - 2 * core
    far = shot - 3 + 6 * core
    column = lax.rem(shot // 2, 2)
    across = shot + 2 - 4 * column
    onward, backward = shot + 4 - 8 * column, shot - 4 + 8 * column
    beside = 1 - 2 * core
    has_left, has_right = slab > 0, slab < slabs - 1
    has_far = (far >= 0) & (far < shots)
    has_down, has_up = shot >= 2, shot < shots - 2
    has_onward = (onward >= 0) & (onward < shots)
    has_backward = (backward >= 0) & (backward < shots)
    inner = pl.ds(PAD, rows)
    mine = pl.ds(HALO, layers)

    def remote(src, dst, send, recv, where):
        return pltpu.make_async_remote_copy(
            src_ref=src, dst_ref=dst, send_sem=send, recv_sem=recv, device_id=where, device_id_type=MESH
        )

    left, right = {"slab": slab - 1}, {"slab": slab + 1}
    down, up = {"shot": shot - 2}, {"shot": shot + 2}
    partners = (
        (has_left, left),
        (has_right, right),
        (has_down, down),
        (has_up, up),
        (has_onward, {"shot": onward}),
        (has_onward, {"shot": onward + beside}),
        (has_backward, {"shot": backward}),
        (has_backward, {"shot": backward + beside}),
        (None, {"shot": sibling}),
    )

    def on(condition, action):
        if condition is None:
            action()
        else:
            pl.when(condition)(action)

    nearby = (nearby_inner, nearby_edges)
    loads = [
        pltpu.make_async_copy(wave_now.at[0], field.at[0, 1, mine, inner], load_sem.at[0]),
        pltpu.make_async_copy(adjoint_now.at[0], field.at[1, 1, mine, inner], load_sem.at[1]),
        pltpu.make_async_copy(wave_prev.at[0], field.at[0, 0, mine, inner], load_sem.at[2]),
        pltpu.make_async_copy(adjoint_prev.at[0], field.at[1, 0, mine, inner], load_sem.at[3]),
        pltpu.make_async_copy(velocity.at[pl.ds(HALO, layers - 2 * HALO)], nearby_inner.at[REACH], load_sem.at[4]),
        pltpu.make_async_copy(velocity.at[pl.ds(0, HALO)], nearby_edges.at[REACH, pl.ds(0, HALO)], load_sem.at[5]),
        pltpu.make_async_copy(
            velocity.at[pl.ds(layers - HALO, HALO)], nearby_edges.at[REACH, pl.ds(HALO, HALO)], load_sem.at[6]),
    ]
    for load in loads:
        load.start()
    tables = [
        pltpu.make_async_copy(table, held, table_sem.at[i])
        for i, (table, held) in enumerate((
            (aperture_start_in, aperture_start),
            (aperture_count_in, aperture_count),
            (source_cells_in, source_cells),
            (wavelet_in, wavelet),
            (receiver_cells_in, receiver_cells),
            (trace_in, trace),
        ))
    ]
    for table in tables:
        table.start()

    def clear(edge):
        for f in range(2):
            for t in range(1, STEPS + 1):
                field[f, t, pl.ds(edge, HALO), inner, :] = jnp.zeros((HALO, rows, depth), jnp.float32)

    pl.when(jnp.logical_not(has_left))(lambda: clear(0))
    pl.when(jnp.logical_not(has_right))(lambda: clear(HALO + layers))

    barrier = pltpu.get_barrier_semaphore()
    for condition, where in partners:
        on(condition, lambda where=where: pl.semaphore_signal(barrier, inc=1, device_id=where, device_id_type=MESH))
    peers = 1
    for condition, _ in partners[:-1]:
        peers = peers + condition.astype(jnp.int32)
    pl.semaphore_wait(barrier, peers)

    def halo_copies(f, t, source):
        lo = source.at[pl.ds(0, HALO)] if t == 0 else field.at[f, t + 1, pl.ds(HALO, HALO), inner]
        hi = source.at[pl.ds(layers - HALO, HALO)] if t == 0 else field.at[f, t + 1, pl.ds(layers, HALO), inner]
        return (
            (has_left, has_right, remote(
                lo, field.at[f, t + 1, pl.ds(HALO + layers, HALO), inner],
                halo_send.at[f, t, 0], halo_recv.at[f, t, 0], left)),
            (has_right, has_left, remote(
                hi, field.at[f, t + 1, pl.ds(0, HALO), inner],
                halo_send.at[f, t, 1], halo_recv.at[f, t, 1], right)),
        )

    sources = (wave_now.at[0], adjoint_now.at[0])
    halos = [[halo_copies(f, t, sources[f]) for t in range(STEPS)] for f in range(2)]

    def start_halos(f, t):
        for to, _, copy in halos[f][t]:
            on(to, copy.start)

    def sent_halos(f, t):
        for to, _, copy in halos[f][t]:
            on(to, copy.wait_send)

    def wait_halos(f, t):
        for _, given, copy in halos[f][t]:
            on(given, copy.wait_recv)

    entry = REACH + 2 - 4 * column

    def block_copies(h):
        def send(i, source, slot, where):
            return remote(nearby[h].at[source], nearby[h].at[slot], block_send.at[h, i], block_recv.at[h, i], {"shot": where})

        return (
            (None, None, send(0, REACH, 2 * REACH - entry, across)),
            (None, None, send(1, REACH, REACH - beside, sibling)),
            (has_far, has_far, send(2, REACH, 6 * (1 - core), far)),
            (None, None, send(3, entry, entry - beside, sibling)),
            (has_onward, has_backward, send(4, entry, 2 * REACH - entry, onward)),
            (has_onward, has_backward, send(5, entry, 2 * REACH - entry - beside, onward + beside)),
        )

    block_sends = [block_copies(h) for h in range(2)]

    def send_blocks(h):
        for i in range(3):
            on(block_sends[h][i][0], block_sends[h][i][2].start)

    def forward_blocks(h):
        block_sends[h][0][2].wait_recv()
        for i in (4, 5, 3):
            on(block_sends[h][i][0], block_sends[h][i][2].start)

    def wait_blocks(h):
        for i in range(1, 6):
            on(block_sends[h][i][1], block_sends[h][i][2].wait_recv)

    for load in loads[4:]:
        load.wait()
    send_blocks(1)
    start_halos(0, 0)

    def clear_rows(i, carry):
        for f in range(2):
            for t in range(1, STEPS + 1):
                field[f, t, HALO + i, pl.ds(0, PAD), :] = jnp.zeros((PAD, depth), jnp.float32)
                field[f, t, HALO + i, pl.ds(PAD + rows, PAD), :] = jnp.zeros((PAD, depth), jnp.float32)
        return carry

    lax.fori_loop(0, layers, clear_rows, 0)
    for h in range(2):
        for j in range(REACH):
            spread[h, j] = jnp.zeros(spread.shape[2:], jnp.float32)
            spread[h, REACH + blocks + j] = jnp.zeros(spread.shape[2:], jnp.float32)

    apart = jnp.abs(
        lax.broadcasted_iota(jnp.int32, (depth, depth), 0) - lax.broadcasted_iota(jnp.int32, (depth, depth), 1)
    )
    operator = jnp.zeros((depth, depth), jnp.float32)
    for k in range(1, HALO + 1):
        operator = jnp.where(apart == k, jnp.float32(stencil_weights[k]), operator)
    op_high = operator.astype(jnp.bfloat16)
    op_low = (operator - op_high.astype(jnp.float32)).astype(jnp.bfloat16)
    for half in range(2):
        depth_op[pl.ds(half * depth, depth), pl.ds(0, depth)] = op_high
        depth_op[pl.ds(half * depth, depth), pl.ds(depth, depth)] = op_low

    forward_blocks(1)

    for table in tables:
        table.wait()
    live_rows = aperture_count[0] * brows
    at_row = lax.broadcasted_iota(jnp.int32, (1, rows, depth), 1)
    live = at_row < live_rows

    def keep(f, t, start, size):
        part = field[f, t, pl.ds(start, size), inner, :]
        field[f, t, pl.ds(start, size), inner, :] = jnp.where(live, part, 0.0)

    for i, (f, t) in enumerate(((0, 1), (1, 1), (0, 0), (1, 0))):
        loads[i].wait()
        lax.fori_loop(0, layers // BLOCK, lambda b, c, f=f, t=t: (keep(f, t, HALO + b * BLOCK, BLOCK), c)[1], 0)

    send_blocks(0)
    start_halos(1, 0)

    at_y = lax.broadcasted_iota(jnp.int32, (PAD, depth), 0)
    at_z = lax.broadcasted_iota(jnp.int32, (PAD, depth), 1)
    first = slab * layers
    for f, (cells, amps) in enumerate(((source_cells, wavelet), (receiver_cells, trace))):
        count = cells.shape[-1]

        def inject(x, carry, f=f, cells=cells, amps=amps, count=count):
            sums = [jnp.zeros((PAD, depth), jnp.float32)] * STEPS
            for s in range(count):
                hit = (at_y == cells[1, 0, s]) & (at_z == cells[2, 0, s])
                here = cells[0, 0, s] == first + x
                for t in range(STEPS):
                    amp = jnp.where(here, amps[0, t, s], 0.0)
                    sums[t] = sums[t] + jnp.where(hit, amp, 0.0)
            for t in range(STEPS):
                injected[f, t, x] = sums[t]
            return carry

        lax.fori_loop(0, layers, inject, 0)

    forward_blocks(0)

    offset = jnp.clip(aperture_start[0] - shot + REACH, 0, REACH)
    parts = (((HALO, layers - 2 * HALO, 0),), ((0, HALO, 0), (layers - HALO, HALO, HALO)))

    def lay_window(h):
        wait_blocks(h)
        for j in range(blocks):
            here = pl.ds(j * brows, brows)
            alive = j * brows < live_rows
            for start, size, at in parts[h]:
                part = nearby[h][offset + j, pl.ds(at, size)]
                imaging[pl.ds(start, size), here, :] = part * jnp.float32(2.0 * time_step * time_step)
                courant[pl.ds(start, size), here, :] = jnp.where(
                    alive, part * part * jnp.float32(time_step * time_step), 0.0
                )

    def advance(f, t, x):
        here = pl.ds(HALO + x, BLOCK)
        now = field[f, t + 1, here, inner, :]
        high = now.astype(jnp.bfloat16)
        low = (now - high.astype(jnp.float32)).astype(jnp.bfloat16)
        both = jnp.concatenate([high, low], axis=-1).reshape(BLOCK * rows, 2 * depth)
        along_z = jnp.dot(both, depth_op[...], preferred_element_type=jnp.float32)
        total = (along_z[:, :depth] + along_z[:, depth:]).reshape(BLOCK, rows, depth)
        total = total + jnp.float32(3.0 * stencil_weights[0]) * now
        for k in range(1, HALO + 1):
            near = field[f, t + 1, pl.ds(HALO + x + k, BLOCK), inner, :]
            near = near + field[f, t + 1, pl.ds(HALO + x - k, BLOCK), inner, :]
            near = near + field[f, t + 1, here, pl.ds(PAD + k, rows), :]
            near = near + field[f, t + 1, here, pl.ds(PAD - k, rows), :]
            total = total + jnp.float32(stencil_weights[k]) * near
        own = pl.ds(x, BLOCK)
        if t == STEPS - 1:
            kept, at, row = (wave_out, adjoint_out)[f].at[0], own, 0
        else:
            kept, at, row = field.at[f, t + 2], here, PAD
        if f == 0:
            image = field[1, t + 1, here, inner, :] * total
            grad[own] = image if t == 0 else grad[own] + image
        later = 2.0 * now - field[f, t, here, inner, :] + courant[own] * total
        kept[at, pl.ds(row, PAD), :] = later[:, :PAD] + injected[f, t, own]
        kept[at, pl.ds(row + PAD, rows - PAD), :] = later[:, PAD:]

    def inside(f, t):
        lax.fori_loop(1, layers // BLOCK - 1, lambda b, c: (advance(f, t, b * BLOCK), c)[1], 0)

    def edges(f, t):
        lax.fori_loop(0, 2, lambda b, c: (advance(f, t, b * (layers - BLOCK)), c)[1], 0)

    def grad_copies(h):
        return (
            remote(to_sibling.at[h], from_sibling.at[h], grad_send.at[h, 0], grad_recv.at[h, 0], {"shot": sibling}),
            remote(to_far.at[h], from_far.at[h], grad_send.at[h, 1], grad_recv.at[h, 1], {"shot": far}),
            remote(to_pair.at[h, 0], from_pair.at[h, 1], grad_send.at[h, 2], grad_recv.at[h, 2], down),
            remote(to_pair.at[h, 1], from_pair.at[h, 0], grad_send.at[h, 3], grad_recv.at[h, 3], up),
        )

    grads = [grad_copies(h) for h in range(2)]
    back = 2 * REACH - offset

    def piece(h, o):
        return spread[h, back + o]

    def send_gradient(h):
        for j in range(blocks):
            here = pl.ds(j * brows, brows)
            for start, size, at in parts[h]:
                own = pl.ds(start, size)
                spread[h, REACH + j, pl.ds(at, size)] = grad[own, here, :] * imaging[own, here, :]
        toward = 1 - 2 * core
        for i, o in enumerate((0, -2, 2)):
            to_sibling[h, i] = piece(h, toward + o)
        grads[h][0].start()
        to_far[h] = piece(h, 6 * core - 3)
        on(has_far, grads[h][1].start)

    def pass_gradient(h):
        grads[h][0].wait_recv()
        to_pair[h, 0] = piece(h, -2) + from_sibling[h, 1]
        to_pair[h, 1] = piece(h, 2) + from_sibling[h, 2]
        on(has_down, grads[h][2].start)
        on(has_up, grads[h][3].start)

    def take_gradient(h):
        total = piece(h, 0) + from_sibling[h, 0]
        on(has_far, grads[h][1].wait_recv)
        on(has_up, grads[h][2].wait_recv)
        on(has_down, grads[h][3].wait_recv)
        total = total + jnp.where(has_far, from_far[h], 0.0)
        total = total + jnp.where(has_down, from_pair[h, 0], 0.0)
        total = total + jnp.where(has_up, from_pair[h, 1], 0.0)
        for start, size, at in parts[h]:
            gradient_out[pl.ds(start, size)] = total[at : at + size]

    def mask_halos(f):
        keep(f, 1, 0, HALO)
        keep(f, 1, HALO + layers, HALO)

    lay_window(1)
    for f in range(2):
        wait_halos(f, 0)
        mask_halos(f)
        edges(f, 0)
        if f:
            sent_halos(0, 1)
        start_halos(f, 1)
    lay_window(0)
    inside(0, 0)
    inside(1, 0)

    for t in range(1, STEPS - 1):
        for f in range(2):
            inside(f, t)
            wait_halos(f, t)
            edges(f, t)
            if f:
                sent_halos(0, t + 1)
            start_halos(f, t + 1)

    t = STEPS - 1
    inside(0, t)
    send_gradient(0)
    inside(1, t)
    wait_halos(0, t)
    pass_gradient(0)
    edges(0, t)
    send_gradient(1)
    pass_gradient(1)
    wait_halos(1, t)
    edges(1, t)
    take_gradient(0)
    take_gradient(1)

    sent_halos(0, 0)
    for t in range(STEPS):
        sent_halos(1, t)
    for h in range(2):
        for to, _, copy in block_sends[h]:
            on(to, copy.wait_send)
    for h in range(2):
        for to, copy in zip((None, has_far, has_down, has_up), grads[h]):
            on(to, copy.wait_send)


def deliver(*refs):
    count = len(refs) // 2
    done = refs[-1]
    copies = [pltpu.make_async_copy(refs[i], refs[count + i], done.at[i]) for i in range(count)]
    for copy in copies:
        copy.start()
    for copy in copies:
        copy.wait()


def per_device(
    velocity,
    aperture_start,
    aperture_count,
    wave_prev,
    wave_now,
    adjoint_prev,
    adjoint_now,
    source_cells,
    wavelet,
    receiver_cells,
    trace,
):
    layers, brows, depth = velocity.shape
    rows = wave_now.shape[2]
    blocks = rows // brows
    block = (layers, brows, depth)
    half = (layers // 2, brows, depth)
    anywhere = pl.BlockSpec(memory_space=pl.ANY)
    f32 = jnp.float32
    out_shape = (
        jax.ShapeDtypeStruct(wave_now.shape, f32),
        jax.ShapeDtypeStruct(wave_now.shape, f32),
        jax.ShapeDtypeStruct(velocity.shape, f32),
    )
    results = pl.pallas_call(
        kernel,
        out_shape=tuple(pltpu.VMEM(leaf.shape, leaf.dtype) for leaf in out_shape),
        in_specs=[anywhere] * 11,
        out_specs=(pl.BlockSpec(memory_space=pltpu.VMEM),) * 3,
        scratch_shapes=[
            pltpu.SMEM(aperture_start.shape, jnp.int32),
            pltpu.SMEM(aperture_count.shape, jnp.int32),
            pltpu.SMEM((3, 1, source_cells.shape[1]), jnp.int32),
            pltpu.SMEM(wavelet.shape, f32),
            pltpu.SMEM((3, 1, receiver_cells.shape[1]), jnp.int32),
            pltpu.SMEM(trace.shape, f32),
            pltpu.VMEM((2, STEPS + 1, layers + 2 * HALO, rows + 2 * PAD, depth), f32),
            pltpu.VMEM((2 * REACH + 1, *half), f32),
            pltpu.VMEM((2 * REACH + 1, *half), f32),
            pltpu.VMEM((layers, rows, depth), f32),
            pltpu.VMEM((layers, rows, depth), f32),
            pltpu.VMEM((layers, rows, depth), f32),
            pltpu.VMEM((2, blocks + 2 * REACH, *half), f32),
            pltpu.VMEM((2, STEPS, layers, PAD, depth), f32),
            pltpu.VMEM((2 * depth, 2 * depth), jnp.bfloat16),
            pltpu.VMEM((2, 3, *half), f32),
            pltpu.VMEM((2, 3, *half), f32),
            pltpu.VMEM((2, *half), f32),
            pltpu.VMEM((2, *half), f32),
            pltpu.VMEM((2, 2, *half), f32),
            pltpu.VMEM((2, 2, *half), f32),
            pltpu.SemaphoreType.DMA((7,)),
            pltpu.SemaphoreType.DMA((6,)),
            pltpu.SemaphoreType.DMA((2, STEPS, 2)),
            pltpu.SemaphoreType.DMA((2, STEPS, 2)),
            pltpu.SemaphoreType.DMA((2, 6)),
            pltpu.SemaphoreType.DMA((2, 6)),
            pltpu.SemaphoreType.DMA((2, 4)),
            pltpu.SemaphoreType.DMA((2, 4)),
        ],
        compiler_params=pltpu.CompilerParams(
            collective_id=0, has_side_effects=True, vmem_limit_bytes=60 * 1024 * 1024
        ),
        name="inversion",
    )(
        velocity,
        aperture_start,
        aperture_count,
        wave_prev,
        wave_now,
        adjoint_prev,
        adjoint_now,
        jnp.transpose(source_cells, (2, 0, 1)),
        wavelet,
        jnp.transpose(receiver_cells, (2, 0, 1)),
        trace,
    )
    return pl.pallas_call(
        deliver,
        out_shape=out_shape,
        in_specs=[pl.BlockSpec(memory_space=pltpu.VMEM)] * 3,
        out_specs=(anywhere,) * 3,
        scratch_shapes=[pltpu.SemaphoreType.DMA((3,))],
        compiler_params=pltpu.CompilerParams(vmem_limit_bytes=1024 * 1024),
        name="deliver",
    )(*results)


def solution(mesh):
    fields = P("shot", "slab", None, None)
    table = P("shot", None, None)
    return jax.shard_map(
        per_device,
        mesh=mesh,
        in_specs=(P("slab", "shot", None), P("shot"), P("shot"), fields, fields, fields, fields, table, table, table, table),
        out_specs=(fields, fields, P("slab", "shot", None)),
        check_vma=False,
    )
```
